128 devices in a mesh: sect: 8 (over z, core), rows: 16 (over x, y).
Axes of the slice: x: 4, y: 4, z: 4, core: 2. Of those that a mesh axis runs over, the one named last changes fastest.
Arguments:
- a_tiles: bfloat16 [2048, 27, 128, 128], P(('sect', 'rows')), may hold values from -0.109375 to 0.109375
- a_cols: int32 [2048, 27], P(('sect', 'rows')), may hold values from 0 to 2047, as said below
- a_count: int32 [2048], P(('sect', 'rows')), may hold values from 1 to 27, as said below
- p_tiles: bfloat16 [2048, 128, 128], P(('sect', 'rows')), may hold values from -0.125 to 0.125
- coarse_map: int32 [2048], P(('sect', 'rows')), may hold values from 0 to 127, as said below
- p_coarse: float32 [16384, 256], P(('sect', 'rows')), may hold values from -0.046875 to 0.046875
Outputs:
- coarse_one: float32 [16384, 2048], P(('sect', 'rows'))
- coarsest: float32 [256, 256], replicated
The draws below stay inside these ranges and needn't reach their ends.
Inputs may be any that keep to these rules, and one draw needn't show every extreme that they name: `a_cols`: slot 0 of each block row names its own block; every column block lies on the same device as its row or on the device one before or after it along rows, in the same section. `a_count`: some block row of every device uses all 27 slots. `coarse_map`: fine block row i of section s aggregates into one of the coarse blocks s * 16 to s * 16 + 15.
All inputs are finite; a program needn't handle non-finite values.
Results may differ from the reference program's by a relative error of at most 0.0029.
Values may be sent and summed in bfloat16 or wider, within the bound.
No kernel may reach another device: no remote copies, remote signals or barrier semaphores. Data moves between devices by JAX's collectives and lax.ppermute only.
A program may use at most 128 MiB of HBM per device.

```python
import jax
import jax.numpy as jnp
from jax import lax

TILE = 128
RB_DEV = 16
KA = 27
CBS = 16
C2 = 256
NF = 2048
NCR = 16384
N_SECT = 8
N_ROWS = 16


def draw_a_cols(key, part):
    key = jax.random.fold_in(key, 11)
    first_key, second_key = jax.random.split(key)
    row_ids = jnp.arange(NF, dtype=jnp.int32)
    device_ids = row_ids // RB_DEV
    position = device_ids % N_ROWS
    offsets = jax.random.randint(first_key, (NF, KA), -1, 2, dtype=jnp.int32)
    target = position[:, None] + offsets
    offsets = jnp.where((target < 0) | (target >= N_ROWS), 0, offsets)
    within = jax.random.randint(second_key, (NF, KA), 0, RB_DEV, dtype=jnp.int32)
    columns = (device_ids[:, None] + offsets) * RB_DEV + within
    slot_ids = jnp.arange(KA, dtype=jnp.int32)[None, :]
    return jnp.where(slot_ids == 0, row_ids[:, None], columns).astype(jnp.int32)


def draw_a_count(key, part):
    key = jax.random.fold_in(key, 23)
    first_key, second_key = jax.random.split(key)
    device_count = NF // RB_DEV
    lowest = jax.random.randint(first_key, (device_count,), 1, KA + 1, dtype=jnp.int32)
    lowest_rows = jnp.repeat(lowest, RB_DEV)
    counts = jax.random.randint(second_key, (NF,), lowest_rows, KA + 1, dtype=jnp.int32)
    row_ids = jnp.arange(NF, dtype=jnp.int32)
    return jnp.where(row_ids % RB_DEV == 0, KA, counts).astype(jnp.int32)


def draw_coarse_map(key, part):
    key = jax.random.fold_in(key, 37)
    row_ids = jnp.arange(NF, dtype=jnp.int32)
    per_section = RB_DEV * N_ROWS
    section = row_ids // per_section
    within = row_ids % per_section
    chosen = jax.random.randint(key, (NF,), 0, CBS, dtype=jnp.int32)
    picked = jnp.where(within < CBS, within, chosen)
    return (section * CBS + picked).astype(jnp.int32)


def level_of(key, shape, cuts, low, top_value):
    gain = 1.0
    for dim, parts in cuts:
        steps = jax.random.uniform(jax.random.fold_in(jax.random.fold_in(key, 6), dim), (parts,), jnp.float32, low / len(cuts), top_value / len(cuts))
        gain = gain * jnp.repeat(jnp.exp(steps), shape[dim] // parts).reshape((-1,) + (1,) * (len(shape) - 1 - dim))
    return gain


def gaussian(key, dims, scale, most, shards=(), held_as=jnp.bfloat16):
    loudness = level_of(key, dims, shards, -0.22, 0.18) if shards else 1.0
    drawn = jax.random.normal(key, dims, jnp.float32) * scale * loudness
    return jnp.minimum(jnp.maximum(drawn, -most), most).astype(held_as)


def setup_inputs(seed: int = 0) -> dict:
    splits = jax.random.split(jax.random.key(seed), 7)
    a_tiles = gaussian(splits[0], (NF, KA, TILE, TILE), (TILE * KA) ** -0.5, 0.109375, ((0, 128),))
    a_cols = draw_a_cols(jax.random.fold_in(splits[6], 71), 0)
    a_count = draw_a_count(jax.random.fold_in(splits[6], 71), 0)
    p_tiles = gaussian(splits[3], (NF, TILE, TILE), (TILE * 16) ** -0.5, 0.125, ((0, 128),))
    coarse_map = draw_coarse_map(jax.random.fold_in(splits[6], 71), 0)
    p_coarse = gaussian(splits[5], (NCR, C2), NCR ** -0.5, 0.046875, ((0, 128),), jnp.float32)
    return dict(a_tiles=a_tiles, a_cols=a_cols, a_count=a_count, p_tiles=p_tiles, coarse_map=coarse_map, p_coarse=p_coarse)


def group_part(index, a_tiles, a_cols, a_count, p_tiles, coarse_map):
    first = index * RB_DEV
    tiles = lax.dynamic_slice_in_dim(a_tiles, first, RB_DEV, 0)
    columns = lax.dynamic_slice_in_dim(a_cols, first, RB_DEV, 0).astype(jnp.int32)
    counts = lax.dynamic_slice_in_dim(a_count, first, RB_DEV, 0)
    own_map = lax.dynamic_slice_in_dim(coarse_map, first, RB_DEV, 0)
    own_tiles = lax.dynamic_slice_in_dim(p_tiles, first, RB_DEV, 0)
    section = index // N_ROWS
    picked = jnp.take(p_tiles, columns, axis=0)
    picked_map = jnp.take(coarse_map, columns, axis=0)
    in_use = jnp.arange(KA, dtype=jnp.int32)[None, :] < counts[:, None]
    products = jnp.einsum("lkij,lkjy->lkiy", tiles.astype(jnp.float32), picked.astype(jnp.float32), precision=lax.Precision.HIGHEST)
    coarse_tiles = jnp.where(in_use[:, :, None, None], products, 0.0).astype(jnp.bfloat16)
    blocks = jnp.arange(CBS, dtype=jnp.int32)
    row_onehot = ((own_map - section * CBS)[:, None] == blocks).astype(jnp.float32)
    col_onehot = ((picked_map - section * CBS)[:, :, None] == blocks).astype(jnp.float32)
    grouped = jnp.einsum("lkb,lkiy->lbiy", col_onehot, coarse_tiles.astype(jnp.float32), precision=lax.Precision.HIGHEST)
    projected = jnp.einsum("lix,lbiy->lbxy", own_tiles.astype(jnp.float32), grouped, precision=lax.Precision.HIGHEST)
    partial_sum = jnp.einsum("la,lbxy->axby", row_onehot, projected, precision=lax.Precision.HIGHEST)
    return partial_sum.reshape(CBS * TILE, CBS * TILE), section


def reference(a_tiles, a_cols, a_count, p_tiles, coarse_map, p_coarse):
    width = CBS * TILE

    def advance(totals, index):
        partial_sum, section = group_part(index, a_tiles, a_cols, a_count, p_tiles, coarse_map)
        rows_at = section * width
        current = lax.dynamic_slice_in_dim(totals, rows_at, width, 0)
        return lax.dynamic_update_slice_in_dim(totals, current + partial_sum, rows_at, 0), None

    start_state = jnp.zeros((NCR, width), jnp.float32)
    coarse_one, _ = lax.scan(advance, start_state, jnp.arange(NF // RB_DEV, dtype=jnp.int32))
    blocks_one = coarse_one.reshape(N_SECT, width, width)
    prolong = p_coarse.reshape(N_SECT, width, C2)
    applied = jnp.einsum("sab,sbc->sac", blocks_one, prolong, precision=lax.Precision.HIGHEST)
    coarsest = jnp.einsum("sad,sac->dc", prolong, applied, precision=lax.Precision.HIGHEST)
    return coarse_one, coarsest
```

```python
import functools

import jax
import jax.numpy as jnp
from jax import lax
from jax.experimental import pallas as pl
from jax.experimental.pallas import tpu as pltpu
from jax.sharding import PartitionSpec as P

CBS = 16
TILE = 128
RB = 16
KA = 27
GROUP = 9
SIDE = 4
WIDTH = CBS * TILE
C2 = 256

HALF_A = (2, 1)
HALF_B = (3, 0)
FAR = [2 * SIDE + dv for dv in HALF_A + HALF_B]
NEXT_ALONE = [1 * SIDE + dv for dv in HALF_B] + [3 * SIDE + dv for dv in HALF_A]
OWN = [0 * SIDE + dv for dv in HALF_A + HALF_B]
NEXT_JOINED = [1 * SIDE + dv for dv in HALF_A] + [3 * SIDE + dv for dv in HALF_B]
SEQUENCE = FAR + NEXT_ALONE + NEXT_JOINED + OWN
PAIRS = len(SEQUENCE) // 2
COUNT, ORDER, STARTS, INFO = KA, KA + 1, KA + 2, KA + 3
Q_SCALE = 2.0**20


def cost(microseconds):
    return pl.CostEstimate(flops=0, bytes_accessed=int(microseconds * 3.7e6), transcendentals=0)


def plan_body(cols, counts, own_map, info, table):
    def fill(i, _):
        for k in range(KA):
            table[i, k] = cols[i, k] - info[4]
        table[i, COUNT] = counts[i]
        table[i, INFO] = info[lax.min(i, 7)]
        return 0

    lax.fori_loop(0, RB, fill, 0)
    first_core = info[1] == 0
    names = []
    for i in range(RB):
        block = own_map[i] - info[0]
        high, low = lax.shift_right_logical(block, 2), lax.bitwise_and(block, 3)
        du = lax.bitwise_and(jnp.where(first_core, high, low) - info[2], 3)
        dv = lax.bitwise_and(jnp.where(first_core, low, high) - info[3], 3)
        names.append(du * SIDE + dv)
    n = jnp.int32(0)
    for j, code in enumerate(SEQUENCE):
        table[j, STARTS] = n
        for i in range(RB):
            table[n, ORDER] = jnp.int32(i)
            n = n + (names[i] == code).astype(jnp.int32)
    table[len(SEQUENCE), STARTS] = n


def row_plan(*operands):
    smem = pl.BlockSpec(memory_space=pltpu.SMEM)
    return pl.pallas_call(
        plan_body,
        out_shape=jax.ShapeDtypeStruct((RB + 1, 32), jnp.int32),
        in_specs=[smem] * len(operands),
        out_specs=smem,
        cost_estimate=cost(3),
    )(*operands)


def galerkin_body(table, maps, a_ref, left_ref, own_ref, right_ref, _, *rest):
    outs, (a_buf, tiles, acc, stage, a_sem, p_sem, out_sem) = rest[:PAIRS], rest[PAIRS:]

    def fetch(r):
        slot = lax.rem(r, 2)
        return pltpu.make_async_copy(a_ref.at[table[r, ORDER]], a_buf.at[slot], a_sem.at[slot])

    fetch(0).start()
    loads = [
        pltpu.make_async_copy(src.at[pl.ds(0, RB)], tiles.at[pl.ds(n * RB, RB)], p_sem.at[n])
        for n, src in enumerate((left_ref, own_ref, right_ref))
    ]
    for load in loads:
        load.start()
    acc[...] = jnp.zeros_like(acc)
    for load in loads:
        load.wait()

    def row(r, _):
        @pl.when(r + 1 < RB)
        def _():
            fetch(r + 1).start()

        fetch(r).wait()
        i = table[r, ORDER]
        slot = lax.rem(r, 2)
        count = table[i, COUNT]
        left = tiles[RB + i].T
        for k in range(0, KA, 2):
            products, places = [], []
            for s in range(k, min(k + 2, KA)):
                col = jnp.clip(table[i, s], 0, 3 * RB - 1)
                block = jnp.clip(maps[lax.shift_right_logical(col, 4), lax.bitwise_and(col, RB - 1)], 0, CBS - 1)
                places.append(pl.multiple_of(jnp.where(s < count, block, CBS) * TILE, TILE))
                products.append(
                    jnp.dot(a_buf[slot, s], tiles[col], preferred_element_type=jnp.float32).astype(jnp.bfloat16)
                )
            terms = jnp.dot(left, jnp.concatenate(products, axis=1), preferred_element_type=jnp.float32)
            for n, place in enumerate(places):
                acc[:, pl.ds(place, TILE)] += terms[:, n * TILE:(n + 1) * TILE]
        return 0

    def leave(n, half):
        return pltpu.make_async_copy(stage.at[half], outs[n].at[half], out_sem.at[half])

    def block(t, _):
        pair, half = lax.div(t, 2), lax.rem(t, 2)
        lax.fori_loop(table[t, STARTS], table[t + 1, STARTS], row, 0)

        @pl.when(pair > 0)
        def _():
            leave(0, half).wait()

        for first in range(0, WIDTH, TILE):
            columns = pl.ds(first, TILE)
            stage[half, :, columns] = acc[:, columns].astype(jnp.bfloat16)
            acc[:, columns] = jnp.zeros((TILE, TILE), jnp.float32)
        for n in range(PAIRS):
            @pl.when(pair == n)
            def _(n=n):
                leave(n, half).start()
        return 0

    lax.fori_loop(0, 2 * PAIRS, block, 0)
    for half in range(2):
        leave(0, half).wait()


def galerkin(table, maps, a_tiles, left, own, right, after_this):
    anywhere = pl.BlockSpec(memory_space=pl.ANY)
    return pl.pallas_call(
        galerkin_body,
        out_shape=[jax.ShapeDtypeStruct((2, TILE, WIDTH), jnp.bfloat16)] * PAIRS,
        grid_spec=pltpu.PrefetchScalarGridSpec(
            num_scalar_prefetch=2,
            grid=(1,),
            in_specs=[pl.BlockSpec(memory_space=pltpu.HBM)] + [anywhere] * 4,
            out_specs=[anywhere] * PAIRS,
            scratch_shapes=[
                pltpu.VMEM((2, KA, TILE, TILE), jnp.bfloat16),
                pltpu.VMEM((3 * RB, TILE, TILE), jnp.bfloat16),
                pltpu.VMEM((TILE, WIDTH + TILE), jnp.float32),
                pltpu.VMEM((2, TILE, WIDTH), jnp.bfloat16),
                pltpu.SemaphoreType.DMA((2,)),
                pltpu.SemaphoreType.DMA((3,)),
                pltpu.SemaphoreType.DMA((2,)),
            ],
        ),
        compiler_params=pltpu.CompilerParams(vmem_limit_bytes=52 * 1024 * 1024),
        cost_estimate=cost(20),
    )(table, maps, a_tiles, left, own, right, after_this)


def coarsest_body(table, *refs):
    parts = refs[:PAIRS]
    high_ref, low_ref, out_ref, right, rest = refs[PAIRS:]
    step = pl.program_id(0)

    def block_at(u, v):
        u, v = lax.bitwise_and(table[2, INFO] + u, 3), lax.bitwise_and(table[3, INFO] + v, 3)
        block = jnp.where(table[1, INFO] == 0, u * SIDE + v, v * SIDE + u)
        return pl.ds(pl.multiple_of(block * TILE, TILE), TILE)

    @pl.when(step == 0)
    def _():
        for n in range(CBS):
            right[block_at(n % SIDE, n // SIDE), :] = high_ref[n]
            rest[block_at(n % SIDE, n // SIDE), :] = low_ref[n]
        out_ref[...] = jnp.zeros_like(out_ref)

    for n, part in enumerate(parts):
        @pl.when(step == n)
        def _(n=n, part=part):
            applied = jnp.dot(part[...].reshape(2 * TILE, WIDTH), right[...], preferred_element_type=jnp.float32)
            high = applied.astype(jnp.bfloat16)
            low = (applied - high.astype(jnp.float32)).astype(jnp.bfloat16)
            places = [block_at(code // SIDE, code % SIDE) for code in SEQUENCE[2 * n:2 * n + 2]]
            left_high = jnp.concatenate([right[place, :] for place in places], axis=0).T
            left_low = jnp.concatenate([rest[place, :] for place in places], axis=0).T
            terms = jnp.dot(left_high, jnp.concatenate([high, low], axis=1), preferred_element_type=jnp.float32)
            out_ref[...] += terms[:, :C2] + (
                terms[:, C2:] + jnp.dot(left_low, high, preferred_element_type=jnp.float32)
            )


def coarsest_term(table, parts, high, low):
    whole = pl.BlockSpec((CBS, TILE, C2), lambda j, *_: (0, 0, 0))
    return pl.pallas_call(
        coarsest_body,
        out_shape=jax.ShapeDtypeStruct((C2, C2), jnp.float32),
        grid_spec=pltpu.PrefetchScalarGridSpec(
            num_scalar_prefetch=1,
            grid=(PAIRS,),
            in_specs=[pl.BlockSpec((2, TILE, WIDTH), lambda j, *_: (0, 0, 0))] * PAIRS + [whole, whole],
            out_specs=pl.BlockSpec((C2, C2), lambda j, *_: (0, 0)),
            scratch_shapes=[pltpu.VMEM((WIDTH, C2), jnp.bfloat16)] * 2,
        ),
        compiler_params=pltpu.CompilerParams(vmem_limit_bytes=52 * 1024 * 1024),
        cost_estimate=cost(6),
    )(table, *parts, high, low)


def joined_body(up, from_far_a, down, from_far_b, _, up_out, down_out):
    up_out[...] = (up[...].astype(jnp.float32) + from_far_a[...].astype(jnp.float32)).astype(jnp.bfloat16)
    down_out[...] = (down[...].astype(jnp.float32) + from_far_b[...].astype(jnp.float32)).astype(jnp.bfloat16)


def joined(up, from_far_a, down, from_far_b, after_this):
    rows = 32
    part = pl.BlockSpec((2, rows, WIDTH), lambda j: (0, j, 0))
    return pl.pallas_call(
        joined_body,
        out_shape=[jax.ShapeDtypeStruct(up.shape, jnp.bfloat16)] * 2,
        grid=(TILE // rows,),
        in_specs=[part] * 4 + [pl.BlockSpec(memory_space=pl.ANY)],
        out_specs=[part] * 2,
        compiler_params=pltpu.CompilerParams(vmem_limit_bytes=32 * 1024 * 1024),
        cost_estimate=cost(2),
    )(up, from_far_a, down, from_far_b, after_this)


def torus_steps():
    def pairs(second, target):
        found = []
        for sect in range(8):
            for row in range(SIDE * SIDE):
                at = [row // SIDE, row % SIDE]
                axis = (sect % 2) ^ second
                at[axis] = target(at[axis])
                found.append((sect * 16 + row, sect * 16 + at[0] * SIDE + at[1]))
        return found

    return [{by: pairs(second, lambda at: (at + by) % SIDE) for by in (1, -1, 2)} for second in (0, 1)]


STEPS = torus_steps()


def send(value, second, by):
    return lax.ppermute(value, ("sect", "rows"), STEPS[second][by])


def wide(value):
    return value.astype(jnp.float32)


def share_out(term):
    pieces = term.reshape(32, 8, 2, 128).transpose(0, 2, 1, 3).reshape(128, 4, 128)
    return jnp.sum(lax.all_to_all(pieces, ("sect", "rows"), 0, 0), axis=0)


def bring_back(piece):
    back = lax.all_to_all(jnp.broadcast_to(piece[None], (128,) + piece.shape), ("sect", "rows"), 0, 0)
    return back.reshape(32, 2, 8, 128).transpose(0, 2, 1, 3).reshape(C2, C2)


def around(value, second):
    return jnp.stack([value, send(value, second, -1), send(value, second, 2), send(value, second, 1)])


def reduced_body(own_a, own_b, up_a, up_b, down_a, down_b, _, far, after, before, mine):
    def total(n, *refs):
        value = refs[0][n].astype(jnp.float32)
        for ref in refs[1:]:
            value = value + ref[n].astype(jnp.float32)
        return value

    far[...] = total(0, own_a, up_a, down_a).astype(jnp.bfloat16)
    after[...] = total(1, own_a, up_a, down_a).astype(jnp.bfloat16)
    before[...] = total(0, own_b, up_b, down_b).astype(jnp.bfloat16)
    mine[...] = total(1, own_b, up_b, down_b)


def reduced(own_a, own_b, up_a, up_b, down_a, down_b, after_this):
    rows = 64
    pair = pl.BlockSpec((2, rows, WIDTH), lambda j: (0, j, 0))
    one = pl.BlockSpec((rows, WIDTH), lambda j: (j, 0))
    shape = (TILE, WIDTH)
    return pl.pallas_call(
        reduced_body,
        out_shape=[jax.ShapeDtypeStruct(shape, jnp.bfloat16)] * 3 + [jax.ShapeDtypeStruct(shape, jnp.float32)],
        grid=(TILE // rows,),
        in_specs=[pair] * 6 + [pl.BlockSpec(memory_space=pl.ANY)],
        out_specs=[one] * 4,
        compiler_params=pltpu.CompilerParams(vmem_limit_bytes=32 * 1024 * 1024),
        cost_estimate=cost(3),
    )(own_a, own_b, up_a, up_b, down_a, down_b, after_this)


def per_device(a_tiles, a_cols, a_count, p_tiles, coarse_map, p_coarse):
    section = lax.axis_index("sect")
    position = lax.axis_index("rows")
    core = lax.rem(section, 2)
    x, y = lax.div(position, SIDE), lax.rem(position, SIDE)
    u, v = jnp.where(core == 0, x, y), jnp.where(core == 0, y, x)
    zero = jnp.zeros_like(core)
    first_row = (section * 16 + position - 1) * RB
    info = jnp.stack([section * CBS, core, u, v, first_row, zero, zero, zero]).astype(jnp.int32)
    up = [(i, i + 1) for i in range(15)]
    down = [(i + 1, i) for i in range(15)]
    local_map = coarse_map - section * CBS
    map_tile = jnp.pad(local_map.astype(jnp.bfloat16)[None, None], ((0, 0), (0, TILE - 1), (0, TILE - RB)))
    own = jnp.concatenate([p_tiles, map_tile], axis=0)
    left, right = lax.ppermute(own, "rows", up), lax.ppermute(own, "rows", down)
    maps = jnp.stack([left[RB, 0, :RB].astype(jnp.int32), local_map, right[RB, 0, :RB].astype(jnp.int32)])

    line = around((p_coarse * Q_SCALE).astype(jnp.float16), 0)
    square = around(line, 1)
    prolong = square.reshape(CBS, TILE, C2).astype(jnp.float32) * (1.0 / Q_SCALE)
    prolong_high = lax.reduce_precision(prolong, 8, 7)
    prolong_low = (prolong - prolong_high).astype(jnp.bfloat16)
    prolong_high = prolong_high.astype(jnp.bfloat16)

    table = row_plan(a_cols, a_count, coarse_map, info)
    all_held = jnp.sum(square[1:, 0, :8, :TILE].astype(jnp.float32), axis=0)
    parts = galerkin(table, maps, a_tiles, left, own, right, all_held)
    far_a, far_b, up_b, down_a, up_a, down_b, own_a, own_b = parts
    from_far_a, from_far_b = send(far_a, 0, 1), send(far_b, 0, -1)
    from_up_b, from_down_a = send(up_b, 0, 1), send(down_a, 0, -1)
    own_term = coarsest_term(table, parts, prolong_high, prolong_low)
    up_a, down_b = joined(up_a, from_far_a, down_b, from_far_b, own_term)
    from_up_a, from_down_b = send(up_a, 0, 1), send(down_b, 0, -1)

    own_piece = share_out(own_term)
    far, after, before, mine = reduced(own_a, own_b, from_up_a, from_up_b, from_down_a, from_down_b, own_piece)
    from_far, from_after, from_before = send(far, 1, 2), send(after, 1, 1), send(before, 1, -1)
    coarsest = bring_back(own_piece)
    owned_rows = mine + (wide(from_far) + (wide(from_after) + wide(from_before)))
    return (owned_rows, coarsest)


def solution(mesh):
    placed = (
        P(("sect", "rows"), None, None, None),
        P(("sect", "rows"), None),
        P(("sect", "rows")),
        P(("sect", "rows"), None, None),
        P(("sect", "rows")),
        P(("sect", "rows"), None),
    )
    return jax.shard_map(
        per_device,
        mesh=mesh,
        in_specs=placed,
        out_specs=(P(("sect", "rows"), None), P()),
        check_vma=False,
    )
```

```python
import functools

import jax
import jax.numpy as jnp
from jax import lax
from jax.experimental import pallas as pl
from jax.experimental.pallas import tpu as pltpu
from jax.sharding import PartitionSpec as P

CBS = 16
TILE = 128
RB = 16
KA = 27
GROUP = 9
SIDE = 4
WIDTH = CBS * TILE
C2 = 256

HALF_A = (2, 1)
HALF_B = (3, 0)
FAR = [2 * SIDE + dv for dv in HALF_A + HALF_B]
NEXT_ALONE = [1 * SIDE + dv for dv in HALF_B] + [3 * SIDE + dv for dv in HALF_A]
OWN = [0 * SIDE + dv for dv in HALF_A + HALF_B]
NEXT_JOINED = [1 * SIDE + dv for dv in HALF_A] + [3 * SIDE + dv for dv in HALF_B]
SEQUENCE = FAR + NEXT_ALONE + NEXT_JOINED + OWN
PAIRS = len(SEQUENCE) // 2
COUNT, ORDER, STARTS, INFO = KA, KA + 1, KA + 2, KA + 3
Q_SCALE = 2.0**20


def cost(microseconds):
    return pl.CostEstimate(flops=0, bytes_accessed=int(microseconds * 3.7e6), transcendentals=0)


def plan_body(cols, counts, own_map, info, table):
    def fill(i, _):
        for k in range(KA):
            table[i, k] = cols[i, k] - info[4]
        table[i, COUNT] = counts[i]
        table[i, INFO] = info[lax.min(i, 7)]
        return 0

    lax.fori_loop(0, RB, fill, 0)
    first_core = info[1] == 0
    names = []
    for i in range(RB):
        block = own_map[i] - info[0]
        high, low = lax.shift_right_logical(block, 2), lax.bitwise_and(block, 3)
        du = lax.bitwise_and(jnp.where(first_core, high, low) - info[2], 3)
        dv = lax.bitwise_and(jnp.where(first_core, low, high) - info[3], 3)
        names.append(du * SIDE + dv)
    n = jnp.int32(0)
    for j, code in enumerate(SEQUENCE):
        table[j, STARTS] = n
        for i in range(RB):
            table[n, ORDER] = jnp.int32(i)
            n = n + (names[i] == code).astype(jnp.int32)
    table[len(SEQUENCE), STARTS] = n


def row_plan(*operands):
    smem = pl.BlockSpec(memory_space=pltpu.SMEM)
    return pl.pallas_call(
        plan_body,
        out_shape=jax.ShapeDtypeStruct((RB + 1, 32), jnp.int32),
        in_specs=[smem] * len(operands),
        out_specs=smem,
        cost_estimate=cost(3),
    )(*operands)


def galerkin_body(table, maps, a_ref, left_ref, own_ref, right_ref, *rest):
    outs, (scale_ref, a_buf, tiles, acc, stage, a_sem, p_sem, out_sem) = rest[:PAIRS], rest[PAIRS:]
    scale_ref[...] = jnp.full(scale_ref.shape, 1.0 / Q_SCALE, jnp.float32)

    def fetch(r):
        slot = lax.rem(r, 2)
        return pltpu.make_async_copy(a_ref.at[table[r, ORDER]], a_buf.at[slot], a_sem.at[slot])

    fetch(0).start()
    loads = [
        pltpu.make_async_copy(src.at[pl.ds(0, RB)], tiles.at[pl.ds(n * RB, RB)], p_sem.at[n])
        for n, src in enumerate((left_ref, own_ref, right_ref))
    ]
    for load in loads:
        load.start()
    acc[...] = jnp.zeros_like(acc)
    for load in loads:
        load.wait()

    def row(r, _):
        @pl.when(r + 1 < RB)
        def _():
            fetch(r + 1).start()

        fetch(r).wait()
        i = table[r, ORDER]
        slot = lax.rem(r, 2)
        count = table[i, COUNT]
        left = tiles[RB + i].T
        for k in range(0, KA, 2):
            products, places = [], []
            for s in range(k, min(k + 2, KA)):
                col = jnp.clip(table[i, s], 0, 3 * RB - 1)
                block = jnp.clip(maps[lax.shift_right_logical(col, 4), lax.bitwise_and(col, RB - 1)], 0, CBS - 1)
                places.append(pl.multiple_of(jnp.where(s < count, block, CBS) * TILE, TILE))
                products.append(
                    jnp.dot(a_buf[slot, s], tiles[col], preferred_element_type=jnp.float32).astype(jnp.bfloat16)
                )
            terms = jnp.dot(left, jnp.concatenate(products, axis=1), preferred_element_type=jnp.float32)
            for n, place in enumerate(places):
                acc[:, pl.ds(place, TILE)] += terms[:, n * TILE:(n + 1) * TILE]
        return 0

    def leave(n, half):
        return pltpu.make_async_copy(stage.at[half], outs[n].at[half], out_sem.at[half])

    def block(t, _):
        pair, half = lax.div(t, 2), lax.rem(t, 2)
        lax.fori_loop(table[t, STARTS], table[t + 1, STARTS], row, 0)

        @pl.when(pair > 0)
        def _():
            leave(0, half).wait()

        for first in range(0, WIDTH, TILE):
            columns = pl.ds(first, TILE)
            stage[half, :, columns] = acc[:, columns].astype(jnp.bfloat16)
            acc[:, columns] = jnp.zeros((TILE, TILE), jnp.float32)
        for n in range(PAIRS):
            @pl.when(pair == n)
            def _(n=n):
                leave(n, half).start()
        return 0

    lax.fori_loop(0, 2 * PAIRS, block, 0)
    for half in range(2):
        leave(0, half).wait()


def galerkin(table, maps, a_tiles, left, own, right):
    anywhere = pl.BlockSpec(memory_space=pl.ANY)
    return pl.pallas_call(
        galerkin_body,
        out_shape=[jax.ShapeDtypeStruct((2, TILE, WIDTH), jnp.bfloat16)] * PAIRS
        + [jax.ShapeDtypeStruct((1, TILE), jnp.float32)],
        grid_spec=pltpu.PrefetchScalarGridSpec(
            num_scalar_prefetch=2,
            grid=(1,),
            in_specs=[pl.BlockSpec(memory_space=pltpu.HBM)] + [anywhere] * 3,
            out_specs=[anywhere] * PAIRS + [pl.BlockSpec((1, TILE), lambda j, *_: (0, 0))],
            scratch_shapes=[
                pltpu.VMEM((2, KA, TILE, TILE), jnp.bfloat16),
                pltpu.VMEM((3 * RB, TILE, TILE), jnp.bfloat16),
                pltpu.VMEM((TILE, WIDTH + TILE), jnp.float32),
                pltpu.VMEM((2, TILE, WIDTH), jnp.bfloat16),
                pltpu.SemaphoreType.DMA((2,)),
                pltpu.SemaphoreType.DMA((3,)),
                pltpu.SemaphoreType.DMA((2,)),
            ],
        ),
        compiler_params=pltpu.CompilerParams(vmem_limit_bytes=52 * 1024 * 1024),
        cost_estimate=cost(20),
    )(table, maps, a_tiles, left, own, right)


def coarsest_body(table, *refs):
    parts = refs[:PAIRS]
    high_ref, low_ref, out_ref, right, rest, held, q_sem, part_sem = refs[PAIRS:]

    def block_at(u, v):
        u, v = lax.bitwise_and(table[2, INFO] + u, 3), lax.bitwise_and(table[3, INFO] + v, 3)
        block = jnp.where(table[1, INFO] == 0, u * SIDE + v, v * SIDE + u)
        return pl.ds(pl.multiple_of(block * TILE, TILE), TILE)

    factors = [
        pltpu.make_async_copy(src.at[n], dst.at[block_at(n % SIDE, n // SIDE)], q_sem.at[m])
        for m, (src, dst) in enumerate(((high_ref, right), (low_ref, rest)))
        for n in range(CBS)
    ]
    loads = [
        pltpu.make_async_copy(part, held.at[pl.ds(2 * n, 2)], part_sem.at[n]) for n, part in enumerate(parts)
    ]
    for copy in factors[:CBS] + loads[:2] + factors[CBS:] + loads[2:]:
        copy.start()
    for m, (src, dst) in enumerate(((high_ref, right), (low_ref, rest))):
        pltpu.make_async_copy(src, dst.reshape(CBS, TILE, C2), q_sem.at[m]).wait()
    total = None
    for n in range(0, PAIRS, 2):
        loads[n].wait()
        loads[n + 1].wait()
        rows = held[2 * n:2 * n + 4].reshape(4 * TILE, WIDTH)
        applied = jnp.dot(rows, right[...], preferred_element_type=jnp.float32)
        high = applied.astype(jnp.bfloat16)
        low = (applied - high.astype(jnp.float32)).astype(jnp.bfloat16)
        places = [block_at(code // SIDE, code % SIDE) for code in SEQUENCE[2 * n:2 * n + 4]]
        left_high = jnp.concatenate([right[place, :] for place in places], axis=0).T
        left_low = jnp.concatenate([rest[place, :] for place in places], axis=0).T
        terms = jnp.dot(left_high, jnp.concatenate([high, low], axis=1), preferred_element_type=jnp.float32)
        term = terms[:, :C2] + (terms[:, C2:] + jnp.dot(left_low, high, preferred_element_type=jnp.float32))
        if n == 0:
            out_ref[...] = term
        else:
            out_ref[...] += term


def coarsest_term(table, parts, high, low):
    return pl.pallas_call(
        coarsest_body,
        out_shape=jax.ShapeDtypeStruct((C2, C2), jnp.float32),
        grid_spec=pltpu.PrefetchScalarGridSpec(
            num_scalar_prefetch=1,
            grid=(1,),
            in_specs=[pl.BlockSpec(memory_space=pl.ANY)] * (PAIRS + 2),
            out_specs=pl.BlockSpec((C2, C2), lambda j, *_: (0, 0)),
            scratch_shapes=[
                pltpu.VMEM((WIDTH, C2), jnp.bfloat16),
                pltpu.VMEM((WIDTH, C2), jnp.bfloat16),
                pltpu.VMEM((2 * PAIRS, TILE, WIDTH), jnp.bfloat16),
                pltpu.SemaphoreType.DMA((2,)),
                pltpu.SemaphoreType.DMA((PAIRS,)),
            ],
        ),
        compiler_params=pltpu.CompilerParams(vmem_limit_bytes=52 * 1024 * 1024),
        cost_estimate=cost(6),
    )(table, *parts, high, low)


def held_back(first, second, after_this):
    anywhere = pl.BlockSpec(memory_space=pl.ANY)
    return pl.pallas_call(
        lambda *refs: None,
        out_shape=[jax.ShapeDtypeStruct(value.shape, value.dtype) for value in (first, second)],
        in_specs=[anywhere] * 3,
        out_specs=[anywhere] * 2,
        input_output_aliases={0: 0, 1: 1},
        cost_estimate=cost(1),
    )(first, second, after_this)


def joined_body(up, from_far_a, down, from_far_b, _, up_out, down_out):
    up_out[...] = (up[...].astype(jnp.float32) + from_far_a[...].astype(jnp.float32)).astype(jnp.bfloat16)
    down_out[...] = (down[...].astype(jnp.float32) + from_far_b[...].astype(jnp.float32)).astype(jnp.bfloat16)


def joined(up, from_far_a, down, from_far_b, after_this):
    rows = 32
    part = pl.BlockSpec((2, rows, WIDTH), lambda j: (0, j, 0))
    return pl.pallas_call(
        joined_body,
        out_shape=[jax.ShapeDtypeStruct(up.shape, jnp.bfloat16)] * 2,
        grid=(TILE // rows,),
        in_specs=[part] * 4 + [pl.BlockSpec(memory_space=pl.ANY)],
        out_specs=[part] * 2,
        compiler_params=pltpu.CompilerParams(vmem_limit_bytes=32 * 1024 * 1024),
        cost_estimate=cost(2),
    )(up, from_far_a, down, from_far_b, after_this)


def torus_steps():
    def pairs(second, target):
        found = []
        for sect in range(8):
            for row in range(SIDE * SIDE):
                at = [row // SIDE, row % SIDE]
                axis = (sect % 2) ^ second
                at[axis] = target(at[axis])
                found.append((sect * 16 + row, sect * 16 + at[0] * SIDE + at[1]))
        return found

    return [{by: pairs(second, lambda at: (at + by) % SIDE) for by in (1, -1, 2)} for second in (0, 1)]


STEPS = torus_steps()


def send(value, second, by):
    return lax.ppermute(value, ("sect", "rows"), STEPS[second][by])


def wide(value):
    return value.astype(jnp.float32)


def share_out(term):
    pieces = term.reshape(32, 8, 2, 128).transpose(0, 2, 1, 3).reshape(128, 4, 128)
    return jnp.sum(lax.all_to_all(pieces, ("sect", "rows"), 0, 0), axis=0)


def bring_back(piece):
    back = lax.all_to_all(jnp.broadcast_to(piece[None], (128,) + piece.shape), ("sect", "rows"), 0, 0)
    return back.reshape(32, 2, 8, 128).transpose(0, 2, 1, 3).reshape(C2, C2)


def around(value, second):
    return jnp.stack([value, send(value, second, -1), send(value, second, 2), send(value, second, 1)])


def reduced_body(own_a, own_b, up_a, up_b, down_a, down_b, _, far, after, before, mine):
    def total(n, *refs):
        value = refs[0][n].astype(jnp.float32)
        for ref in refs[1:]:
            value = value + ref[n].astype(jnp.float32)
        return value

    far[...] = total(0, own_a, up_a, down_a).astype(jnp.bfloat16)
    after[...] = total(1, own_a, up_a, down_a).astype(jnp.bfloat16)
    before[...] = total(0, own_b, up_b, down_b).astype(jnp.bfloat16)
    mine[...] = total(1, own_b, up_b, down_b)


def reduced(own_a, own_b, up_a, up_b, down_a, down_b, after_this):
    rows = 64
    pair = pl.BlockSpec((2, rows, WIDTH), lambda j: (0, j, 0))
    one = pl.BlockSpec((rows, WIDTH), lambda j: (j, 0))
    shape = (TILE, WIDTH)
    return pl.pallas_call(
        reduced_body,
        out_shape=[jax.ShapeDtypeStruct(shape, jnp.bfloat16)] * 3 + [jax.ShapeDtypeStruct(shape, jnp.float32)],
        grid=(TILE // rows,),
        in_specs=[pair] * 6 + [pl.BlockSpec(memory_space=pl.ANY)],
        out_specs=[one] * 4,
        compiler_params=pltpu.CompilerParams(vmem_limit_bytes=32 * 1024 * 1024),
        cost_estimate=cost(3),
    )(own_a, own_b, up_a, up_b, down_a, down_b, after_this)


def per_device(a_tiles, a_cols, a_count, p_tiles, coarse_map, p_coarse):
    section = lax.axis_index("sect")
    position = lax.axis_index("rows")
    core = lax.rem(section, 2)
    x, y = lax.div(position, SIDE), lax.rem(position, SIDE)
    u, v = jnp.where(core == 0, x, y), jnp.where(core == 0, y, x)
    zero = jnp.zeros_like(core)
    first_row = (section * 16 + position - 1) * RB
    info = jnp.stack([section * CBS, core, u, v, first_row, zero, zero, zero]).astype(jnp.int32)
    up = [(i, i + 1) for i in range(15)]
    down = [(i + 1, i) for i in range(15)]
    local_map = coarse_map - section * CBS
    map_tile = jnp.pad(local_map.astype(jnp.bfloat16)[None, None], ((0, 0), (0, TILE - 1), (0, TILE - RB)))
    own = jnp.concatenate([p_tiles, map_tile], axis=0)
    left, right = lax.ppermute(own, "rows", up), lax.ppermute(own, "rows", down)
    maps = jnp.stack([left[RB, 0, :RB].astype(jnp.int32), local_map, right[RB, 0, :RB].astype(jnp.int32)])

    line = around((p_coarse * Q_SCALE).astype(jnp.float16), 0)
    square = around(line, 1)
    table = row_plan(a_cols, a_count, coarse_map, info)
    *parts, scale = galerkin(table, maps, a_tiles, left, own, right)
    far_a, far_b, up_b, down_a, up_a, down_b, own_a, own_b = parts
    prolong = square.reshape(CBS, TILE, C2).astype(jnp.float32) * scale[0, 0]
    prolong_high = lax.reduce_precision(prolong, 8, 7)
    prolong_low = (prolong - prolong_high).astype(jnp.bfloat16)
    prolong_high = prolong_high.astype(jnp.bfloat16)
    far_a, far_b = held_back(far_a, far_b, prolong_high)
    parts = (far_a, far_b, up_b, down_a, up_a, down_b, own_a, own_b)
    from_far_a, from_far_b = send(far_a, 0, 1), send(far_b, 0, -1)
    from_up_b, from_down_a = send(up_b, 0, 1), send(down_a, 0, -1)
    own_term = coarsest_term(table, parts, prolong_high, prolong_low)
    up_a, down_b = joined(up_a, from_far_a, down_b, from_far_b, own_term)
    from_up_a, from_down_b = send(up_a, 0, 1), send(down_b, 0, -1)

    own_piece = share_out(own_term)
    far, after, before, mine = reduced(own_a, own_b, from_up_a, from_up_b, from_down_a, from_down_b, own_piece)
    from_far, from_after, from_before = send(far, 1, 2), send(after, 1, 1), send(before, 1, -1)
    coarsest = bring_back(own_piece)
    owned_rows = mine + (wide(from_far) + (wide(from_after) + wide(from_before)))
    return (owned_rows, coarsest)


def solution(mesh):
    placed = (
        P(("sect", "rows"), None, None, None),
        P(("sect", "rows"), None),
        P(("sect", "rows")),
        P(("sect", "rows"), None, None),
        P(("sect", "rows")),
        P(("sect", "rows"), None),
    )
    return jax.shard_map(
        per_device,
        mesh=mesh,
        in_specs=placed,
        out_specs=(P(("sect", "rows"), None), P()),
        check_vma=False,
    )
```

```python
import functools

import jax
import jax.numpy as jnp
from jax import lax
from jax.experimental import pallas as pl
from jax.experimental.pallas import tpu as pltpu
from jax.sharding import PartitionSpec as P

CBS = 16
TILE = 128
RB = 16
KA = 27
GROUP = 1
SIDE = 4
WIDTH = CBS * TILE
C2 = 256

HALF_A = (2, 1)
HALF_B = (3, 0)
FAR = [2 * SIDE + dv for dv in HALF_A + HALF_B]
NEXT_ALONE = [1 * SIDE + dv for dv in HALF_B] + [3 * SIDE + dv for dv in HALF_A]
OWN = [0 * SIDE + dv for dv in HALF_A + HALF_B]
NEXT_JOINED = [1 * SIDE + dv for dv in HALF_A] + [3 * SIDE + dv for dv in HALF_B]
SEQUENCE = FAR + NEXT_ALONE + NEXT_JOINED + OWN
PAIRS = len(SEQUENCE) // 2
COUNT, ORDER, STARTS, INFO = KA, KA + 1, KA + 2, KA + 3
Q_SCALE = 2.0**20


def cost(microseconds):
    return pl.CostEstimate(flops=0, bytes_accessed=int(microseconds * 3.7e6), transcendentals=0)


def plan_body(cols, counts, own_map, info, table):
    def fill(i, _):
        for k in range(KA):
            table[i, k] = cols[i, k] - info[4]
        table[i, COUNT] = counts[i]
        table[i, INFO] = info[lax.min(i, 7)]
        return 0

    lax.fori_loop(0, RB, fill, 0)
    first_core = info[1] == 0
    names = []
    for i in range(RB):
        block = own_map[i] - info[0]
        high, low = lax.shift_right_logical(block, 2), lax.bitwise_and(block, 3)
        du = lax.bitwise_and(jnp.where(first_core, high, low) - info[2], 3)
        dv = lax.bitwise_and(jnp.where(first_core, low, high) - info[3], 3)
        names.append(du * SIDE + dv)
    n = jnp.int32(0)
    for j, code in enumerate(SEQUENCE):
        table[j, STARTS] = n
        for i in range(RB):
            table[n, ORDER] = jnp.int32(i)
            n = n + (names[i] == code).astype(jnp.int32)
    table[len(SEQUENCE), STARTS] = n


def row_plan(*operands):
    smem = pl.BlockSpec(memory_space=pltpu.SMEM)
    return pl.pallas_call(
        plan_body,
        out_shape=jax.ShapeDtypeStruct((RB + 1, 32), jnp.int32),
        in_specs=[smem] * len(operands),
        out_specs=smem,
        cost_estimate=cost(3),
    )(*operands)


def galerkin_body(table, maps, a_ref, left_ref, own_ref, right_ref, *rest):
    outs, (scale_ref, a_buf, tiles, acc, stage, a_sem, p_sem, out_sem) = rest[:PAIRS], rest[PAIRS:]
    scale_ref[...] = jnp.full(scale_ref.shape, 1.0 / Q_SCALE, jnp.float32)

    def fetch(r):
        slot = lax.rem(r, 2)
        return pltpu.make_async_copy(a_ref.at[table[r, ORDER]], a_buf.at[slot], a_sem.at[slot])

    fetch(0).start()
    loads = [
        pltpu.make_async_copy(src.at[pl.ds(0, RB)], tiles.at[pl.ds(n * RB, RB)], p_sem.at[n])
        for n, src in enumerate((left_ref, own_ref, right_ref))
    ]
    for load in loads:
        load.start()
    acc[...] = jnp.zeros_like(acc)
    for load in loads:
        load.wait()

    def row(r, _):
        @pl.when(r + 1 < RB)
        def _():
            fetch(r + 1).start()

        fetch(r).wait()
        i = table[r, ORDER]
        slot = lax.rem(r, 2)
        count = table[i, COUNT]
        left = tiles[RB + i].T
        for k in range(0, KA, GROUP):
            products, places = [], []
            for s in range(k, min(k + GROUP, KA)):
                col = jnp.clip(table[i, s], 0, 3 * RB - 1)
                block = jnp.clip(maps[lax.shift_right_logical(col, 4), lax.bitwise_and(col, RB - 1)], 0, CBS - 1)
                places.append(pl.multiple_of(jnp.where(s < count, block, CBS) * TILE, TILE))
                products.append(
                    jnp.dot(a_buf[slot, s], tiles[col], preferred_element_type=jnp.float32).astype(jnp.bfloat16)
                )
            terms = jnp.dot(left, jnp.concatenate(products, axis=1) if len(products) > 1 else products[0], preferred_element_type=jnp.float32)
            for n, place in enumerate(places):
                acc[:, pl.ds(place, TILE)] += terms[:, n * TILE:(n + 1) * TILE]
        return 0

    def leave(n, half):
        return pltpu.make_async_copy(stage.at[half], outs[n].at[half], out_sem.at[half])

    def block(t, _):
        pair, half = lax.div(t, 2), lax.rem(t, 2)
        lax.fori_loop(table[t, STARTS], table[t + 1, STARTS], row, 0)

        @pl.when(pair > 0)
        def _():
            leave(0, half).wait()

        for first in range(0, WIDTH, TILE):
            columns = pl.ds(first, TILE)
            stage[half, :, columns] = acc[:, columns].astype(jnp.bfloat16)
            acc[:, columns] = jnp.zeros((TILE, TILE), jnp.float32)
        for n in range(PAIRS):
            @pl.when(pair == n)
            def _(n=n):
                leave(n, half).start()
        return 0

    lax.fori_loop(0, 2 * PAIRS, block, 0)
    for half in range(2):
        leave(0, half).wait()


def galerkin(table, maps, a_tiles, left, own, right):
    anywhere = pl.BlockSpec(memory_space=pl.ANY)
    return pl.pallas_call(
        galerkin_body,
        out_shape=[jax.ShapeDtypeStruct((2, TILE, WIDTH), jnp.bfloat16)] * PAIRS
        + [jax.ShapeDtypeStruct((1, TILE), jnp.float32)],
        grid_spec=pltpu.PrefetchScalarGridSpec(
            num_scalar_prefetch=2,
            grid=(1,),
            in_specs=[pl.BlockSpec(memory_space=pltpu.HBM)] + [anywhere] * 3,
            out_specs=[anywhere] * PAIRS + [pl.BlockSpec((1, TILE), lambda j, *_: (0, 0))],
            scratch_shapes=[
                pltpu.VMEM((2, KA, TILE, TILE), jnp.bfloat16),
                pltpu.VMEM((3 * RB, TILE, TILE), jnp.bfloat16),
                pltpu.VMEM((TILE, WIDTH + TILE), jnp.float32),
                pltpu.VMEM((2, TILE, WIDTH), jnp.bfloat16),
                pltpu.SemaphoreType.DMA((2,)),
                pltpu.SemaphoreType.DMA((3,)),
                pltpu.SemaphoreType.DMA((2,)),
            ],
        ),
        compiler_params=pltpu.CompilerParams(vmem_limit_bytes=52 * 1024 * 1024),
        cost_estimate=cost(20),
    )(table, maps, a_tiles, left, own, right)


def coarsest_body(table, *refs):
    parts = refs[:PAIRS]
    high_ref, low_ref, out_ref, right, rest, left, left_rest, applied, applied_rest, held, q_sem, part_sem = refs[PAIRS:]

    def block_at(u, v):
        u, v = lax.bitwise_and(table[2, INFO] + u, 3), lax.bitwise_and(table[3, INFO] + v, 3)
        block = jnp.where(table[1, INFO] == 0, u * SIDE + v, v * SIDE + u)
        return pl.ds(pl.multiple_of(block * TILE, TILE), TILE)

    factors = [
        pltpu.make_async_copy(src.at[n], dst.at[block_at(n % SIDE, n // SIDE)], q_sem.at[m])
        for m, (src, dst) in enumerate(((high_ref, right), (low_ref, rest)))
        for n in range(CBS)
    ]
    loads = [
        pltpu.make_async_copy(part, held.at[pl.ds(2 * n, 2)], part_sem.at[n]) for n, part in enumerate(parts)
    ]
    for copy in factors[:CBS] + loads[:2] + factors[CBS:]:
        copy.start()
    for m, (src, dst) in enumerate(((high_ref, right), (low_ref, rest))):
        pltpu.make_async_copy(src, dst.reshape(CBS, TILE, C2), q_sem.at[m]).wait()
    for n, code in enumerate(SEQUENCE):
        place, columns = block_at(code // SIDE, code % SIDE), pl.ds(n * TILE, TILE)
        left[:, columns] = right[place, :].T
        left_rest[:, columns] = rest[place, :].T
    for n in range(PAIRS):
        loads[n].wait()
        if n + 2 < PAIRS:
            loads[n + 2].start()
        for m in (2 * n, 2 * n + 1):
            value = jnp.dot(held[m], right[...], preferred_element_type=jnp.float32)
            high = value.astype(jnp.bfloat16)
            rows = pl.ds(m * TILE, TILE)
            applied[rows, :] = high
            applied_rest[rows, :] = (value - high.astype(jnp.float32)).astype(jnp.bfloat16)
    for first in range(0, C2, TILE):
        rows = pl.ds(first, TILE)
        term = jnp.dot(left[rows, :], applied[...], preferred_element_type=jnp.float32)
        term += jnp.dot(left[rows, :], applied_rest[...], preferred_element_type=jnp.float32)
        term += jnp.dot(left_rest[rows, :], applied[...], preferred_element_type=jnp.float32)
        out_ref[rows, :] = term


def coarsest_term(table, parts, high, low):
    return pl.pallas_call(
        coarsest_body,
        out_shape=jax.ShapeDtypeStruct((C2, C2), jnp.float32),
        grid_spec=pltpu.PrefetchScalarGridSpec(
            num_scalar_prefetch=1,
            grid=(1,),
            in_specs=[pl.BlockSpec(memory_space=pl.ANY)] * (PAIRS + 2),
            out_specs=pl.BlockSpec((C2, C2), lambda j, *_: (0, 0)),
            scratch_shapes=[
                pltpu.VMEM((WIDTH, C2), jnp.bfloat16),
                pltpu.VMEM((WIDTH, C2), jnp.bfloat16),
                pltpu.VMEM((C2, WIDTH), jnp.bfloat16),
                pltpu.VMEM((C2, WIDTH), jnp.bfloat16),
                pltpu.VMEM((WIDTH, C2), jnp.bfloat16),
                pltpu.VMEM((WIDTH, C2), jnp.bfloat16),
                pltpu.VMEM((2 * PAIRS, TILE, WIDTH), jnp.bfloat16),
                pltpu.SemaphoreType.DMA((2,)),
                pltpu.SemaphoreType.DMA((PAIRS,)),
            ],
        ),
        compiler_params=pltpu.CompilerParams(vmem_limit_bytes=52 * 1024 * 1024),
        cost_estimate=cost(6),
    )(table, *parts, high, low)


def held_back(first, second, after_this):
    anywhere = pl.BlockSpec(memory_space=pl.ANY)
    return pl.pallas_call(
        lambda *refs: None,
        out_shape=[jax.ShapeDtypeStruct(value.shape, value.dtype) for value in (first, second)],
        in_specs=[anywhere] * 3,
        out_specs=[anywhere] * 2,
        input_output_aliases={0: 0, 1: 1},
        cost_estimate=cost(1),
    )(first, second, after_this)


def joined_body(up, from_far_a, down, from_far_b, _, up_out, down_out):
    up_out[...] = (up[...].astype(jnp.float32) + from_far_a[...].astype(jnp.float32)).astype(jnp.bfloat16)
    down_out[...] = (down[...].astype(jnp.float32) + from_far_b[...].astype(jnp.float32)).astype(jnp.bfloat16)


def joined(up, from_far_a, down, from_far_b, after_this):
    rows = 32
    part = pl.BlockSpec((2, rows, WIDTH), lambda j: (0, j, 0))
    return pl.pallas_call(
        joined_body,
        out_shape=[jax.ShapeDtypeStruct(up.shape, jnp.bfloat16)] * 2,
        grid=(TILE // rows,),
        in_specs=[part] * 4 + [pl.BlockSpec(memory_space=pl.ANY)],
        out_specs=[part] * 2,
        compiler_params=pltpu.CompilerParams(vmem_limit_bytes=32 * 1024 * 1024),
        cost_estimate=cost(2),
    )(up, from_far_a, down, from_far_b, after_this)


def torus_steps():
    def pairs(second, target):
        found = []
        for sect in range(8):
            for row in range(SIDE * SIDE):
                at = [row // SIDE, row % SIDE]
                axis = (sect % 2) ^ second
                at[axis] = target(at[axis])
                found.append((sect * 16 + row, sect * 16 + at[0] * SIDE + at[1]))
        return found

    return [{by: pairs(second, lambda at: (at + by) % SIDE) for by in (1, -1, 2)} for second in (0, 1)]


STEPS = torus_steps()


def send(value, second, by):
    return lax.ppermute(value, ("sect", "rows"), STEPS[second][by])


def wide(value):
    return value.astype(jnp.float32)


def share_out(term):
    pieces = term.reshape(32, 8, 2, 128).transpose(0, 2, 1, 3).reshape(128, 4, 128)
    return jnp.sum(lax.all_to_all(pieces, ("sect", "rows"), 0, 0), axis=0)


def bring_back(piece):
    back = lax.all_to_all(jnp.broadcast_to(piece[None], (128,) + piece.shape), ("sect", "rows"), 0, 0)
    return back.reshape(32, 2, 8, 128).transpose(0, 2, 1, 3).reshape(C2, C2)


def around(value, second):
    return jnp.stack([value, send(value, second, -1), send(value, second, 2), send(value, second, 1)])


def reduced_body(own_a, own_b, up_a, up_b, down_a, down_b, _, far, after, before, mine):
    def total(n, *refs):
        value = refs[0][n].astype(jnp.float32)
        for ref in refs[1:]:
            value = value + ref[n].astype(jnp.float32)
        return value

    far[...] = total(0, own_a, up_a, down_a).astype(jnp.bfloat16)
    after[...] = total(1, own_a, up_a, down_a).astype(jnp.bfloat16)
    before[...] = total(0, own_b, up_b, down_b).astype(jnp.bfloat16)
    mine[...] = total(1, own_b, up_b, down_b)


def reduced(own_a, own_b, up_a, up_b, down_a, down_b, after_this):
    rows = 64
    pair = pl.BlockSpec((2, rows, WIDTH), lambda j: (0, j, 0))
    one = pl.BlockSpec((rows, WIDTH), lambda j: (j, 0))
    shape = (TILE, WIDTH)
    return pl.pallas_call(
        reduced_body,
        out_shape=[jax.ShapeDtypeStruct(shape, jnp.bfloat16)] * 3 + [jax.ShapeDtypeStruct(shape, jnp.float32)],
        grid=(TILE // rows,),
        in_specs=[pair] * 6 + [pl.BlockSpec(memory_space=pl.ANY)],
        out_specs=[one] * 4,
        compiler_params=pltpu.CompilerParams(vmem_limit_bytes=32 * 1024 * 1024),
        cost_estimate=cost(3),
    )(own_a, own_b, up_a, up_b, down_a, down_b, after_this)


def per_device(a_tiles, a_cols, a_count, p_tiles, coarse_map, p_coarse):
    section = lax.axis_index("sect")
    position = lax.axis_index("rows")
    core = lax.rem(section, 2)
    x, y = lax.div(position, SIDE), lax.rem(position, SIDE)
    u, v = jnp.where(core == 0, x, y), jnp.where(core == 0, y, x)
    zero = jnp.zeros_like(core)
    first_row = (section * 16 + position - 1) * RB
    info = jnp.stack([section * CBS, core, u, v, first_row, zero, zero, zero]).astype(jnp.int32)
    up = [(i, i + 1) for i in range(15)]
    down = [(i + 1, i) for i in range(15)]
    local_map = coarse_map - section * CBS
    map_tile = jnp.pad(local_map.astype(jnp.bfloat16)[None, None], ((0, 0), (0, TILE - 1), (0, TILE - RB)))
    own = jnp.concatenate([p_tiles, map_tile], axis=0)
    left, right = lax.ppermute(own, "rows", up), lax.ppermute(own, "rows", down)
    maps = jnp.stack([left[RB, 0, :RB].astype(jnp.int32), local_map, right[RB, 0, :RB].astype(jnp.int32)])

    line = around((p_coarse * Q_SCALE).astype(jnp.float16), 0)
    square = around(line, 1)
    table = row_plan(a_cols, a_count, coarse_map, info)
    *parts, scale = galerkin(table, maps, a_tiles, left, own, right)
    far_a, far_b, up_b, down_a, up_a, down_b, own_a, own_b = parts
    prolong = square.reshape(CBS, TILE, C2).astype(jnp.float32) * scale[0, 0]
    prolong_high = lax.reduce_precision(prolong, 8, 7)
    prolong_low = (prolong - prolong_high).astype(jnp.bfloat16)
    prolong_high = prolong_high.astype(jnp.bfloat16)
    far_a, far_b = held_back(far_a, far_b, prolong_high)
    parts = (far_a, far_b, up_b, down_a, up_a, down_b, own_a, own_b)
    from_far_a, from_far_b = send(far_a, 0, 1), send(far_b, 0, -1)
    from_up_b, from_down_a = send(up_b, 0, 1), send(down_a, 0, -1)
    own_term = coarsest_term(table, parts, prolong_high, prolong_low)
    up_a, down_b = joined(up_a, from_far_a, down_b, from_far_b, own_term)
    from_up_a, from_down_b = send(up_a, 0, 1), send(down_b, 0, -1)

    own_piece = share_out(own_term)
    far, after, before, mine = reduced(own_a, own_b, from_up_a, from_up_b, from_down_a, from_down_b, own_piece)
    from_far, from_after, from_before = send(far, 1, 2), send(after, 1, 1), send(before, 1, -1)
    coarsest = bring_back(own_piece)
    owned_rows = mine + (wide(from_far) + (wide(from_after) + wide(from_before)))
    return (owned_rows, coarsest)


def solution(mesh):
    placed = (
        P(("sect", "rows"), None, None, None),
        P(("sect", "rows"), None),
        P(("sect", "rows")),
        P(("sect", "rows"), None, None),
        P(("sect", "rows")),
        P(("sect", "rows"), None),
    )
    return jax.shard_map(
        per_device,
        mesh=mesh,
        in_specs=placed,
        out_specs=(P(("sect", "rows"), None), P()),
        check_vma=False,
    )
```

```python
import functools

import jax
import jax.numpy as jnp
from jax import lax
from jax.experimental import pallas as pl
from jax.experimental.pallas import tpu as pltpu
from jax.sharding import PartitionSpec as P

CBS = 16
TILE = 128
RB = 16
KA = 27
SIDE = 4
WIDTH = CBS * TILE
C2 = 256

HALF_A = (2, 1)
HALF_B = (3, 0)
FAR = [2 * SIDE + dv for dv in HALF_A + HALF_B]
NEXT_ALONE = [1 * SIDE + dv for dv in HALF_B] + [3 * SIDE + dv for dv in HALF_A]
OWN = [0 * SIDE + dv for dv in HALF_A + HALF_B]
NEXT_JOINED = [1 * SIDE + dv for dv in HALF_A] + [3 * SIDE + dv for dv in HALF_B]
SEQUENCE = FAR + NEXT_ALONE + NEXT_JOINED + OWN
PAIRS = len(SEQUENCE) // 2
COUNT, ORDER, STARTS, INFO = KA, KA + 1, KA + 2, KA + 3
Q_SCALE = 2.0**20


def cost(microseconds):
    return pl.CostEstimate(flops=0, bytes_accessed=int(microseconds * 3.7e6), transcendentals=0)


def plan_body(cols, counts, own_map, info, table):
    def fill(i, _):
        for k in range(KA):
            table[i, k] = cols[i, k] - info[4]
        table[i, COUNT] = counts[i]
        table[i, INFO] = info[lax.min(i, 7)]
        return 0

    lax.fori_loop(0, RB, fill, 0)
    first_core = info[1] == 0
    names = []
    for i in range(RB):
        block = own_map[i] - info[0]
        high, low = lax.shift_right_logical(block, 2), lax.bitwise_and(block, 3)
        du = lax.bitwise_and(jnp.where(first_core, high, low) - info[2], 3)
        dv = lax.bitwise_and(jnp.where(first_core, low, high) - info[3], 3)
        names.append(du * SIDE + dv)
    n = jnp.int32(0)
    for j, code in enumerate(SEQUENCE):
        table[j, STARTS] = n
        for i in range(RB):
            table[n, ORDER] = jnp.int32(i)
            n = n + (names[i] == code).astype(jnp.int32)
    table[len(SEQUENCE), STARTS] = n


def row_plan(*operands):
    smem = pl.BlockSpec(memory_space=pltpu.SMEM)
    return pl.pallas_call(
        plan_body,
        out_shape=jax.ShapeDtypeStruct((RB + 1, 32), jnp.int32),
        in_specs=[smem] * len(operands),
        out_specs=smem,
        cost_estimate=cost(3),
    )(*operands)


def galerkin_body(table, maps, a_ref, left_ref, own_ref, right_ref, *rest):
    outs, (scale_ref, a_buf, tiles, acc, stage, a_sem, p_sem, out_sem) = rest[:PAIRS], rest[PAIRS:]
    scale_ref[...] = jnp.full(scale_ref.shape, 1.0 / Q_SCALE, jnp.float32)

    def fetch(r):
        slot = lax.rem(r, 2)
        return pltpu.make_async_copy(a_ref.at[table[r, ORDER]], a_buf.at[slot], a_sem.at[slot])

    fetch(0).start()
    loads = [
        pltpu.make_async_copy(src.at[pl.ds(0, RB)], tiles.at[pl.ds(n * RB, RB)], p_sem.at[n])
        for n, src in enumerate((left_ref, own_ref, right_ref))
    ]
    for load in loads:
        load.start()
    acc[...] = jnp.zeros_like(acc)
    for load in loads:
        load.wait()

    def row(r, _):
        @pl.when(r + 1 < RB)
        def _():
            fetch(r + 1).start()

        fetch(r).wait()
        i = table[r, ORDER]
        slot = lax.rem(r, 2)
        count = table[i, COUNT]
        left = tiles[RB + i].T
        for k in range(0, KA, 2):
            terms, places = [], []
            for s in range(k, min(k + 2, KA)):
                col = jnp.clip(table[i, s], 0, 3 * RB - 1)
                block = jnp.clip(maps[lax.shift_right_logical(col, 4), lax.bitwise_and(col, RB - 1)], 0, CBS - 1)
                places.append(pl.multiple_of(jnp.where(s < count, block, CBS) * TILE, TILE))
                product = jnp.dot(a_buf[slot, s], tiles[col], preferred_element_type=jnp.float32).astype(jnp.bfloat16)
                terms.append(jnp.dot(left, product, preferred_element_type=jnp.float32))
            columns = [pl.ds(place, TILE) for place in places]
            held = [acc[:, column] for column in columns]
            first = held[0] + terms[0]
            if len(columns) == 2:
                second = jnp.where(places[0] == places[1], first, held[1]) + terms[1]
            acc[:, columns[0]] = first
            if len(columns) == 2:
                acc[:, columns[1]] = second
        return 0

    def leave(n, half):
        return pltpu.make_async_copy(stage.at[half], outs[n].at[half], out_sem.at[half])

    def block(t, _):
        pair, half = lax.div(t, 2), lax.rem(t, 2)
        lax.fori_loop(table[t, STARTS], table[t + 1, STARTS], row, 0)

        @pl.when(pair > 0)
        def _():
            leave(0, half).wait()

        for first in range(0, WIDTH, TILE):
            columns = pl.ds(first, TILE)
            stage[half, :, columns] = acc[:, columns].astype(jnp.bfloat16)
            acc[:, columns] = jnp.zeros((TILE, TILE), jnp.float32)
        for n in range(PAIRS):
            @pl.when(pair == n)
            def _(n=n):
                leave(n, half).start()
        return 0

    lax.fori_loop(0, 2 * PAIRS, block, 0)
    for half in range(2):
        leave(0, half).wait()


def galerkin(table, maps, a_tiles, left, own, right):
    anywhere = pl.BlockSpec(memory_space=pl.ANY)
    return pl.pallas_call(
        galerkin_body,
        out_shape=[jax.ShapeDtypeStruct((2, TILE, WIDTH), jnp.bfloat16)] * PAIRS
        + [jax.ShapeDtypeStruct((1, TILE), jnp.float32)],
        grid_spec=pltpu.PrefetchScalarGridSpec(
            num_scalar_prefetch=2,
            grid=(1,),
            in_specs=[pl.BlockSpec(memory_space=pltpu.HBM)] + [anywhere] * 3,
            out_specs=[anywhere] * PAIRS + [pl.BlockSpec((1, TILE), lambda j, *_: (0, 0))],
            scratch_shapes=[
                pltpu.VMEM((2, KA, TILE, TILE), jnp.bfloat16),
                pltpu.VMEM((3 * RB, TILE, TILE), jnp.bfloat16),
                pltpu.VMEM((TILE, WIDTH + TILE), jnp.float32),
                pltpu.VMEM((2, TILE, WIDTH), jnp.bfloat16),
                pltpu.SemaphoreType.DMA((2,)),
                pltpu.SemaphoreType.DMA((3,)),
                pltpu.SemaphoreType.DMA((2,)),
            ],
        ),
        compiler_params=pltpu.CompilerParams(vmem_limit_bytes=52 * 1024 * 1024),
        cost_estimate=cost(20),
    )(table, maps, a_tiles, left, own, right)


def coarsest_body(table, *refs):
    parts = refs[:PAIRS]
    high_ref, low_ref, out_ref, right, rest, left, left_rest, applied, applied_rest, held, q_sem, part_sem = refs[PAIRS:]

    def block_at(u, v):
        u, v = lax.bitwise_and(table[2, INFO] + u, 3), lax.bitwise_and(table[3, INFO] + v, 3)
        block = jnp.where(table[1, INFO] == 0, u * SIDE + v, v * SIDE + u)
        return pl.ds(pl.multiple_of(block * TILE, TILE), TILE)

    factors = [
        pltpu.make_async_copy(src.at[n], dst.at[block_at(n % SIDE, n // SIDE)], q_sem.at[m])
        for m, (src, dst) in enumerate(((high_ref, right), (low_ref, rest)))
        for n in range(CBS)
    ]
    loads = [
        pltpu.make_async_copy(part, held.at[pl.ds(2 * n, 2)], part_sem.at[n]) for n, part in enumerate(parts)
    ]
    for copy in factors[:CBS] + loads[:2] + factors[CBS:]:
        copy.start()
    for m, (src, dst) in enumerate(((high_ref, right), (low_ref, rest))):
        pltpu.make_async_copy(src, dst.reshape(CBS, TILE, C2), q_sem.at[m]).wait()
    for n, code in enumerate(SEQUENCE):
        place, columns = block_at(code // SIDE, code % SIDE), pl.ds(n * TILE, TILE)
        left[:, columns] = right[place, :].T
        left_rest[:, columns] = rest[place, :].T
    for n in range(PAIRS):
        loads[n].wait()
        if n + 2 < PAIRS:
            loads[n + 2].start()
        for m in (2 * n, 2 * n + 1):
            value = jnp.dot(held[m], right[...], preferred_element_type=jnp.float32)
            high = value.astype(jnp.bfloat16)
            rows = pl.ds(m * TILE, TILE)
            applied[rows, :] = high
            applied_rest[rows, :] = (value - high.astype(jnp.float32)).astype(jnp.bfloat16)
    for first in range(0, C2, TILE):
        rows = pl.ds(first, TILE)
        term = jnp.dot(left[rows, :], applied[...], preferred_element_type=jnp.float32)
        term += jnp.dot(left[rows, :], applied_rest[...], preferred_element_type=jnp.float32)
        term += jnp.dot(left_rest[rows, :], applied[...], preferred_element_type=jnp.float32)
        out_ref[rows, :] = term


def coarsest_term(table, parts, high, low):
    return pl.pallas_call(
        coarsest_body,
        out_shape=jax.ShapeDtypeStruct((C2, C2), jnp.float32),
        grid_spec=pltpu.PrefetchScalarGridSpec(
            num_scalar_prefetch=1,
            grid=(1,),
            in_specs=[pl.BlockSpec(memory_space=pl.ANY)] * (PAIRS + 2),
            out_specs=pl.BlockSpec((C2, C2), lambda j, *_: (0, 0)),
            scratch_shapes=[
                pltpu.VMEM((WIDTH, C2), jnp.bfloat16),
                pltpu.VMEM((WIDTH, C2), jnp.bfloat16),
                pltpu.VMEM((C2, WIDTH), jnp.bfloat16),
                pltpu.VMEM((C2, WIDTH), jnp.bfloat16),
                pltpu.VMEM((WIDTH, C2), jnp.bfloat16),
                pltpu.VMEM((WIDTH, C2), jnp.bfloat16),
                pltpu.VMEM((2 * PAIRS, TILE, WIDTH), jnp.bfloat16),
                pltpu.SemaphoreType.DMA((2,)),
                pltpu.SemaphoreType.DMA((PAIRS,)),
            ],
        ),
        compiler_params=pltpu.CompilerParams(vmem_limit_bytes=52 * 1024 * 1024),
        cost_estimate=cost(6),
    )(table, *parts, high, low)


def held_back(first, second, after_this):
    anywhere = pl.BlockSpec(memory_space=pl.ANY)
    return pl.pallas_call(
        lambda *refs: None,
        out_shape=[jax.ShapeDtypeStruct(value.shape, value.dtype) for value in (first, second)],
        in_specs=[anywhere] * 3,
        out_specs=[anywhere] * 2,
        input_output_aliases={0: 0, 1: 1},
        cost_estimate=cost(1),
    )(first, second, after_this)


def joined_body(up, from_far_a, down, from_far_b, _, up_out, down_out):
    up_out[...] = (up[...].astype(jnp.float32) + from_far_a[...].astype(jnp.float32)).astype(jnp.bfloat16)
    down_out[...] = (down[...].astype(jnp.float32) + from_far_b[...].astype(jnp.float32)).astype(jnp.bfloat16)


def joined(up, from_far_a, down, from_far_b, after_this):
    rows = 32
    part = pl.BlockSpec((2, rows, WIDTH), lambda j: (0, j, 0))
    return pl.pallas_call(
        joined_body,
        out_shape=[jax.ShapeDtypeStruct(up.shape, jnp.bfloat16)] * 2,
        grid=(TILE // rows,),
        in_specs=[part] * 4 + [pl.BlockSpec(memory_space=pl.ANY)],
        out_specs=[part] * 2,
        compiler_params=pltpu.CompilerParams(vmem_limit_bytes=32 * 1024 * 1024),
        cost_estimate=cost(2),
    )(up, from_far_a, down, from_far_b, after_this)


def torus_steps():
    def pairs(second, target):
        found = []
        for sect in range(8):
            for row in range(SIDE * SIDE):
                at = [row // SIDE, row % SIDE]
                axis = (sect % 2) ^ second
                at[axis] = target(at[axis])
                found.append((sect * 16 + row, sect * 16 + at[0] * SIDE + at[1]))
        return found

    return [{by: pairs(second, lambda at: (at + by) % SIDE) for by in (1, -1, 2)} for second in (0, 1)]


STEPS = torus_steps()


def send(value, second, by):
    return lax.ppermute(value, ("sect", "rows"), STEPS[second][by])


def wide(value):
    return value.astype(jnp.float32)


def share_out(term):
    pieces = term.reshape(32, 8, 2, 128).transpose(0, 2, 1, 3).reshape(128, 4, 128)
    return jnp.sum(lax.all_to_all(pieces, ("sect", "rows"), 0, 0), axis=0)


def bring_back(piece):
    back = lax.all_to_all(jnp.broadcast_to(piece[None], (128,) + piece.shape), ("sect", "rows"), 0, 0)
    return back.reshape(32, 2, 8, 128).transpose(0, 2, 1, 3).reshape(C2, C2)


def around(value, second):
    return jnp.stack([value, send(value, second, -1), send(value, second, 2), send(value, second, 1)])


def reduced_body(own_a, own_b, up_a, up_b, down_a, down_b, _, far, after, before, mine):
    def total(n, *refs):
        value = refs[0][n].astype(jnp.float32)
        for ref in refs[1:]:
            value = value + ref[n].astype(jnp.float32)
        return value

    far[...] = total(0, own_a, up_a, down_a).astype(jnp.bfloat16)
    after[...] = total(1, own_a, up_a, down_a).astype(jnp.bfloat16)
    before[...] = total(0, own_b, up_b, down_b).astype(jnp.bfloat16)
    mine[...] = total(1, own_b, up_b, down_b)


def reduced(own_a, own_b, up_a, up_b, down_a, down_b, after_this):
    rows = 64
    pair = pl.BlockSpec((2, rows, WIDTH), lambda j: (0, j, 0))
    one = pl.BlockSpec((rows, WIDTH), lambda j: (j, 0))
    shape = (TILE, WIDTH)
    return pl.pallas_call(
        reduced_body,
        out_shape=[jax.ShapeDtypeStruct(shape, jnp.bfloat16)] * 3 + [jax.ShapeDtypeStruct(shape, jnp.float32)],
        grid=(TILE // rows,),
        in_specs=[pair] * 6 + [pl.BlockSpec(memory_space=pl.ANY)],
        out_specs=[one] * 4,
        compiler_params=pltpu.CompilerParams(vmem_limit_bytes=32 * 1024 * 1024),
        cost_estimate=cost(3),
    )(own_a, own_b, up_a, up_b, down_a, down_b, after_this)


def per_device(a_tiles, a_cols, a_count, p_tiles, coarse_map, p_coarse):
    section = lax.axis_index("sect")
    position = lax.axis_index("rows")
    core = lax.rem(section, 2)
    x, y = lax.div(position, SIDE), lax.rem(position, SIDE)
    u, v = jnp.where(core == 0, x, y), jnp.where(core == 0, y, x)
    zero = jnp.zeros_like(core)
    first_row = (section * 16 + position - 1) * RB
    info = jnp.stack([section * CBS, core, u, v, first_row, zero, zero, zero]).astype(jnp.int32)
    up = [(i, i + 1) for i in range(15)]
    down = [(i + 1, i) for i in range(15)]
    local_map = coarse_map - section * CBS
    map_tile = jnp.pad(local_map.astype(jnp.bfloat16)[None, None], ((0, 0), (0, TILE - 1), (0, TILE - RB)))
    own = jnp.concatenate([p_tiles, map_tile], axis=0)
    left, right = lax.ppermute(own, "rows", up), lax.ppermute(own, "rows", down)
    maps = jnp.stack([left[RB, 0, :RB].astype(jnp.int32), local_map, right[RB, 0, :RB].astype(jnp.int32)])

    line = around((p_coarse * Q_SCALE).astype(jnp.float16), 0)
    square = around(line, 1)
    table = row_plan(a_cols, a_count, coarse_map, info)
    *parts, scale = galerkin(table, maps, a_tiles, left, own, right)
    far_a, far_b, up_b, down_a, up_a, down_b, own_a, own_b = parts
    prolong = square.reshape(CBS, TILE, C2).astype(jnp.float32) * scale[0, 0]
    prolong_high = lax.reduce_precision(prolong, 8, 7)
    prolong_low = (prolong - prolong_high).astype(jnp.bfloat16)
    prolong_high = prolong_high.astype(jnp.bfloat16)
    far_a, far_b = held_back(far_a, far_b, prolong_high)
    parts = (far_a, far_b, up_b, down_a, up_a, down_b, own_a, own_b)
    from_far_a, from_far_b = send(far_a, 0, 1), send(far_b, 0, -1)
    own_term = coarsest_term(table, parts, prolong_high, prolong_low)
    up_b, down_a = held_back(up_b, down_a, own_term)
    from_up_b, from_down_a = send(up_b, 0, 1), send(down_a, 0, -1)
    up_a, down_b = joined(up_a, from_far_a, down_b, from_far_b, own_term)
    from_up_a, from_down_b = send(up_a, 0, 1), send(down_b, 0, -1)

    own_piece = share_out(own_term)
    far, after, before, mine = reduced(own_a, own_b, from_up_a, from_up_b, from_down_a, from_down_b, own_piece)
    from_far, from_after, from_before = send(far, 1, 2), send(after, 1, 1), send(before, 1, -1)
    coarsest = bring_back(own_piece)
    owned_rows = mine + (wide(from_far) + (wide(from_after) + wide(from_before)))
    return (owned_rows, coarsest)


def solution(mesh):
    placed = (
        P(("sect", "rows"), None, None, None),
        P(("sect", "rows"), None),
        P(("sect", "rows")),
        P(("sect", "rows"), None, None),
        P(("sect", "rows")),
        P(("sect", "rows"), None),
    )
    return jax.shard_map(
        per_device,
        mesh=mesh,
        in_specs=placed,
        out_specs=(P(("sect", "rows"), None), P()),
        check_vma=False,
    )
```

```python
import functools

import jax
import jax.numpy as jnp
from jax import lax
from jax.experimental import pallas as pl
from jax.experimental.pallas import tpu as pltpu
from jax.sharding import PartitionSpec as P

CBS = 16
TILE = 128
RB = 16
KA = 27
GROUP = 2
AHEAD = 3
CUTS = 3
SIDE = 4
WIDTH = CBS * TILE
C2 = 256

HALF_A = (2, 1)
HALF_B = (3, 0)
FAR = [2 * SIDE + dv for dv in HALF_A + HALF_B]
NEXT_ALONE = [1 * SIDE + dv for dv in HALF_B] + [3 * SIDE + dv for dv in HALF_A]
OWN = [0 * SIDE + dv for dv in HALF_A + HALF_B]
NEXT_JOINED = [1 * SIDE + dv for dv in HALF_A] + [3 * SIDE + dv for dv in HALF_B]
SEQUENCE = FAR + NEXT_ALONE + NEXT_JOINED + OWN
PAIRS = len(SEQUENCE) // 2
COUNT, ORDER, STARTS, INFO = KA, KA + 1, KA + 2, KA + 3
Q_SCALE = 2.0**20


def cost(microseconds):
    return pl.CostEstimate(flops=0, bytes_accessed=int(microseconds * 3.7e6), transcendentals=0)


def plan_body(cols, counts, own_map, info, table):
    def fill(i, _):
        for k in range(KA):
            table[i, k] = cols[i, k] - info[4]
        table[i, COUNT] = counts[i]
        table[i, INFO] = info[lax.min(i, 7)]
        return 0

    lax.fori_loop(0, RB, fill, 0)
    first_core = info[1] == 0
    names = []
    for i in range(RB):
        block = own_map[i] - info[0]
        high, low = lax.shift_right_logical(block, 2), lax.bitwise_and(block, 3)
        du = lax.bitwise_and(jnp.where(first_core, high, low) - info[2], 3)
        dv = lax.bitwise_and(jnp.where(first_core, low, high) - info[3], 3)
        names.append(du * SIDE + dv)
    n = jnp.int32(0)
    for j, code in enumerate(SEQUENCE):
        table[j, STARTS] = n
        for i in range(RB):
            table[n, ORDER] = jnp.int32(i)
            n = n + (names[i] == code).astype(jnp.int32)
    table[len(SEQUENCE), STARTS] = n


def row_plan(*operands):
    smem = pl.BlockSpec(memory_space=pltpu.SMEM)
    return pl.pallas_call(
        plan_body,
        out_shape=jax.ShapeDtypeStruct((RB + 1, 32), jnp.int32),
        in_specs=[smem] * len(operands),
        out_specs=smem,
        cost_estimate=cost(3),
    )(*operands)


def galerkin_body(table, maps, a_ref, left_ref, own_ref, right_ref, *rest):
    outs, (scale_ref, a_buf, tiles, acc, stage, a_sem, p_sem, out_sem) = rest[:PAIRS], rest[PAIRS:]
    scale_ref[...] = jnp.full(scale_ref.shape, 1.0 / Q_SCALE, jnp.float32)

    def fetch(r):
        slot = lax.rem(r, AHEAD + 1)
        part = KA // CUTS
        return [
            pltpu.make_async_copy(
                a_ref.at[table[r, ORDER], pl.ds(n * part, part)], a_buf.at[slot, pl.ds(n * part, part)], a_sem.at[slot, n]
            )
            for n in range(CUTS)
        ]

    for r in range(AHEAD):
        for copy in fetch(r):
            copy.start()
    loads = [
        pltpu.make_async_copy(src.at[pl.ds(0, RB)], tiles.at[pl.ds(n * RB, RB)], p_sem.at[n])
        for n, src in enumerate((left_ref, own_ref, right_ref))
    ]
    for load in loads:
        load.start()
    acc[...] = jnp.zeros_like(acc)
    for load in loads:
        load.wait()

    def row(r, _):
        @pl.when(r + AHEAD < RB)
        def _():
            for copy in fetch(r + AHEAD):
                copy.start()

        for copy in fetch(r):
            copy.wait()
        i = table[r, ORDER]
        slot = lax.rem(r, AHEAD + 1)
        count = table[i, COUNT]
        left = tiles[RB + i].T
        for k in range(0, KA, GROUP):
            products, places = [], []
            for s in range(k, min(k + GROUP, KA)):
                col = jnp.clip(table[i, s], 0, 3 * RB - 1)
                block = jnp.clip(maps[lax.shift_right_logical(col, 4), lax.bitwise_and(col, RB - 1)], 0, CBS - 1)
                places.append(pl.multiple_of(jnp.where(s < count, block, CBS) * TILE, TILE))
                products.append(
                    jnp.dot(a_buf[slot, s], tiles[col], preferred_element_type=jnp.float32).astype(jnp.bfloat16)
                )
            terms = jnp.dot(left, jnp.concatenate(products, axis=1) if len(products) > 1 else products[0], preferred_element_type=jnp.float32)
            for n, place in enumerate(places):
                acc[:, pl.ds(place, TILE)] += terms[:, n * TILE:(n + 1) * TILE]
        return 0

    def leave(n, half):
        return pltpu.make_async_copy(stage.at[half], outs[n].at[half], out_sem.at[half])

    def block(t, _):
        pair, half = lax.div(t, 2), lax.rem(t, 2)
        lax.fori_loop(table[t, STARTS], table[t + 1, STARTS], row, 0)

        @pl.when(pair > 0)
        def _():
            leave(0, half).wait()

        for first in range(0, WIDTH, TILE):
            columns = pl.ds(first, TILE)
            stage[half, :, columns] = acc[:, columns].astype(jnp.bfloat16)
            acc[:, columns] = jnp.zeros((TILE, TILE), jnp.float32)
        for n in range(PAIRS):
            @pl.when(pair == n)
            def _(n=n):
                leave(n, half).start()
        return 0

    lax.fori_loop(0, 2 * PAIRS, block, 0)
    for half in range(2):
        leave(0, half).wait()


def galerkin(table, maps, a_tiles, left, own, right):
    anywhere = pl.BlockSpec(memory_space=pl.ANY)
    return pl.pallas_call(
        galerkin_body,
        out_shape=[jax.ShapeDtypeStruct((2, TILE, WIDTH), jnp.bfloat16)] * PAIRS
        + [jax.ShapeDtypeStruct((1, TILE), jnp.float32)],
        grid_spec=pltpu.PrefetchScalarGridSpec(
            num_scalar_prefetch=2,
            grid=(1,),
            in_specs=[pl.BlockSpec(memory_space=pltpu.HBM)] + [anywhere] * 3,
            out_specs=[anywhere] * PAIRS + [pl.BlockSpec((1, TILE), lambda j, *_: (0, 0))],
            scratch_shapes=[
                pltpu.VMEM((AHEAD + 1, KA, TILE, TILE), jnp.bfloat16),
                pltpu.VMEM((3 * RB, TILE, TILE), jnp.bfloat16),
                pltpu.VMEM((TILE, WIDTH + TILE), jnp.float32),
                pltpu.VMEM((2, TILE, WIDTH), jnp.bfloat16),
                pltpu.SemaphoreType.DMA((AHEAD + 1, CUTS)),
                pltpu.SemaphoreType.DMA((3,)),
                pltpu.SemaphoreType.DMA((2,)),
            ],
        ),
        compiler_params=pltpu.CompilerParams(vmem_limit_bytes=52 * 1024 * 1024),
        cost_estimate=cost(20),
    )(table, maps, a_tiles, left, own, right)


def coarsest_body(table, *refs):
    parts = refs[:PAIRS]
    high_ref, low_ref, out_ref, right, rest, left, left_rest, applied, applied_rest, held, q_sem, part_sem = refs[PAIRS:]

    def block_at(u, v):
        u, v = lax.bitwise_and(table[2, INFO] + u, 3), lax.bitwise_and(table[3, INFO] + v, 3)
        block = jnp.where(table[1, INFO] == 0, u * SIDE + v, v * SIDE + u)
        return pl.ds(pl.multiple_of(block * TILE, TILE), TILE)

    factors = [
        pltpu.make_async_copy(src.at[n], dst.at[block_at(n % SIDE, n // SIDE)], q_sem.at[m])
        for m, (src, dst) in enumerate(((high_ref, right), (low_ref, rest)))
        for n in range(CBS)
    ]
    loads = [
        pltpu.make_async_copy(part, held.at[pl.ds(2 * n, 2)], part_sem.at[n]) for n, part in enumerate(parts)
    ]
    for copy in factors[:CBS] + loads[:4] + factors[CBS:]:
        copy.start()
    for m, (src, dst) in enumerate(((high_ref, right), (low_ref, rest))):
        pltpu.make_async_copy(src, dst.reshape(CBS, TILE, C2), q_sem.at[m]).wait()
    for n, code in enumerate(SEQUENCE):
        place, columns = block_at(code // SIDE, code % SIDE), pl.ds(n * TILE, TILE)
        left[:, columns] = right[place, :].T
        left_rest[:, columns] = rest[place, :].T
    for n in range(PAIRS):
        loads[n].wait()
        if n + 4 < PAIRS:
            loads[n + 4].start()
        for m in (2 * n, 2 * n + 1):
            value = jnp.dot(held[m], right[...], preferred_element_type=jnp.float32)
            high = value.astype(jnp.bfloat16)
            rows = pl.ds(m * TILE, TILE)
            applied[rows, :] = high
            applied_rest[rows, :] = (value - high.astype(jnp.float32)).astype(jnp.bfloat16)
    for first in range(0, C2, TILE):
        rows = pl.ds(first, TILE)
        term = jnp.dot(left[rows, :], applied[...], preferred_element_type=jnp.float32)
        term += jnp.dot(left[rows, :], applied_rest[...], preferred_element_type=jnp.float32)
        term += jnp.dot(left_rest[rows, :], applied[...], preferred_element_type=jnp.float32)
        out_ref[rows, :] = term


def coarsest_term(table, parts, high, low):
    return pl.pallas_call(
        coarsest_body,
        out_shape=jax.ShapeDtypeStruct((C2, C2), jnp.float32),
        grid_spec=pltpu.PrefetchScalarGridSpec(
            num_scalar_prefetch=1,
            grid=(1,),
            in_specs=[pl.BlockSpec(memory_space=pl.ANY)] * (PAIRS + 2),
            out_specs=pl.BlockSpec((C2, C2), lambda j, *_: (0, 0)),
            scratch_shapes=[
                pltpu.VMEM((WIDTH, C2), jnp.bfloat16),
                pltpu.VMEM((WIDTH, C2), jnp.bfloat16),
                pltpu.VMEM((C2, WIDTH), jnp.bfloat16),
                pltpu.VMEM((C2, WIDTH), jnp.bfloat16),
                pltpu.VMEM((WIDTH, C2), jnp.bfloat16),
                pltpu.VMEM((WIDTH, C2), jnp.bfloat16),
                pltpu.VMEM((2 * PAIRS, TILE, WIDTH), jnp.bfloat16),
                pltpu.SemaphoreType.DMA((2,)),
                pltpu.SemaphoreType.DMA((PAIRS,)),
            ],
        ),
        compiler_params=pltpu.CompilerParams(vmem_limit_bytes=52 * 1024 * 1024),
        cost_estimate=cost(6),
    )(table, *parts, high, low)


def held_back(first, second, after_this):
    anywhere = pl.BlockSpec(memory_space=pl.ANY)
    return pl.pallas_call(
        lambda *refs: None,
        out_shape=[jax.ShapeDtypeStruct(value.shape, value.dtype) for value in (first, second)],
        in_specs=[anywhere] * 3,
        out_specs=[anywhere] * 2,
        input_output_aliases={0: 0, 1: 1},
        cost_estimate=cost(1),
    )(first, second, after_this)


def joined_body(up, from_far_a, down, from_far_b, _, up_out, down_out):
    up_out[...] = (up[...].astype(jnp.float32) + from_far_a[...].astype(jnp.float32)).astype(jnp.bfloat16)
    down_out[...] = (down[...].astype(jnp.float32) + from_far_b[...].astype(jnp.float32)).astype(jnp.bfloat16)


def joined(up, from_far_a, down, from_far_b, after_this):
    rows = 32
    part = pl.BlockSpec((2, rows, WIDTH), lambda j: (0, j, 0))
    return pl.pallas_call(
        joined_body,
        out_shape=[jax.ShapeDtypeStruct(up.shape, jnp.bfloat16)] * 2,
        grid=(TILE // rows,),
        in_specs=[part] * 4 + [pl.BlockSpec(memory_space=pl.ANY)],
        out_specs=[part] * 2,
        compiler_params=pltpu.CompilerParams(vmem_limit_bytes=32 * 1024 * 1024),
        cost_estimate=cost(2),
    )(up, from_far_a, down, from_far_b, after_this)


def torus_steps():
    def pairs(second, target):
        found = []
        for sect in range(8):
            for row in range(SIDE * SIDE):
                at = [row // SIDE, row % SIDE]
                axis = (sect % 2) ^ second
                at[axis] = target(at[axis])
                found.append((sect * 16 + row, sect * 16 + at[0] * SIDE + at[1]))
        return found

    return [{by: pairs(second, lambda at: (at + by) % SIDE) for by in (1, -1, 2)} for second in (0, 1)]


STEPS = torus_steps()


def send(value, second, by):
    return lax.ppermute(value, ("sect", "rows"), STEPS[second][by])


def wide(value):
    return value.astype(jnp.float32)


def share_out(term):
    pieces = term.reshape(32, 8, 2, 128).transpose(0, 2, 1, 3).reshape(128, 4, 128)
    return jnp.sum(lax.all_to_all(pieces, ("sect", "rows"), 0, 0), axis=0)


def bring_back(piece):
    back = lax.all_to_all(jnp.broadcast_to(piece[None], (128,) + piece.shape), ("sect", "rows"), 0, 0)
    return back.reshape(32, 2, 8, 128).transpose(0, 2, 1, 3).reshape(C2, C2)


def around(value, second):
    return jnp.stack([value, send(value, second, -1), send(value, second, 2), send(value, second, 1)])


def reduced_body(own_a, own_b, up_a, up_b, down_a, down_b, _, far, after, before, mine):
    def total(n, *refs):
        value = refs[0][n].astype(jnp.float32)
        for ref in refs[1:]:
            value = value + ref[n].astype(jnp.float32)
        return value

    far[...] = total(0, own_a, up_a, down_a).astype(jnp.bfloat16)
    after[...] = total(1, own_a, up_a, down_a).astype(jnp.bfloat16)
    before[...] = total(0, own_b, up_b, down_b).astype(jnp.bfloat16)
    mine[...] = total(1, own_b, up_b, down_b)


def reduced(own_a, own_b, up_a, up_b, down_a, down_b, after_this):
    rows = 64
    pair = pl.BlockSpec((2, rows, WIDTH), lambda j: (0, j, 0))
    one = pl.BlockSpec((rows, WIDTH), lambda j: (j, 0))
    shape = (TILE, WIDTH)
    return pl.pallas_call(
        reduced_body,
        out_shape=[jax.ShapeDtypeStruct(shape, jnp.bfloat16)] * 3 + [jax.ShapeDtypeStruct(shape, jnp.float32)],
        grid=(TILE // rows,),
        in_specs=[pair] * 6 + [pl.BlockSpec(memory_space=pl.ANY)],
        out_specs=[one] * 4,
        compiler_params=pltpu.CompilerParams(vmem_limit_bytes=32 * 1024 * 1024),
        cost_estimate=cost(3),
    )(own_a, own_b, up_a, up_b, down_a, down_b, after_this)


def per_device(a_tiles, a_cols, a_count, p_tiles, coarse_map, p_coarse):
    section = lax.axis_index("sect")
    position = lax.axis_index("rows")
    core = lax.rem(section, 2)
    x, y = lax.div(position, SIDE), lax.rem(position, SIDE)
    u, v = jnp.where(core == 0, x, y), jnp.where(core == 0, y, x)
    zero = jnp.zeros_like(core)
    first_row = (section * 16 + position - 1) * RB
    info = jnp.stack([section * CBS, core, u, v, first_row, zero, zero, zero]).astype(jnp.int32)
    up = [(i, i + 1) for i in range(15)]
    down = [(i + 1, i) for i in range(15)]
    local_map = coarse_map - section * CBS
    map_tile = jnp.pad(local_map.astype(jnp.bfloat16)[None, None], ((0, 0), (0, TILE - 1), (0, TILE - RB)))
    own = jnp.concatenate([p_tiles, map_tile], axis=0)
    left, right = lax.ppermute(own, "rows", up), lax.ppermute(own, "rows", down)
    maps = jnp.stack([left[RB, 0, :RB].astype(jnp.int32), local_map, right[RB, 0, :RB].astype(jnp.int32)])

    line = around((p_coarse * Q_SCALE).astype(jnp.float16), 0)
    square = around(line, 1)
    table = row_plan(a_cols, a_count, coarse_map, info)
    *parts, scale = galerkin(table, maps, a_tiles, left, own, right)
    far_a, far_b, up_b, down_a, up_a, down_b, own_a, own_b = parts
    prolong = square.reshape(CBS, TILE, C2).astype(jnp.float32) * scale[0, 0]
    prolong_high = lax.reduce_precision(prolong, 8, 7)
    prolong_low = (prolong - prolong_high).astype(jnp.bfloat16)
    prolong_high = prolong_high.astype(jnp.bfloat16)
    far_a, far_b = held_back(far_a, far_b, prolong_high)
    parts = (far_a, far_b, up_b, down_a, up_a, down_b, own_a, own_b)
    from_far_a, from_far_b = send(far_a, 0, 1), send(far_b, 0, -1)
    from_up_b, from_down_a = send(up_b, 0, 1), send(down_a, 0, -1)
    own_term = coarsest_term(table, parts, prolong_high, prolong_low)
    up_a, down_b = joined(up_a, from_far_a, down_b, from_far_b, own_term)
    from_up_a, from_down_b = send(up_a, 0, 1), send(down_b, 0, -1)

    own_piece = share_out(own_term)
    far, after, before, mine = reduced(own_a, own_b, from_up_a, from_up_b, from_down_a, from_down_b, own_piece)
    from_far, from_after, from_before = send(far, 1, 2), send(after, 1, 1), send(before, 1, -1)
    coarsest = bring_back(own_piece)
    owned_rows = mine + (wide(from_far) + (wide(from_after) + wide(from_before)))
    return (owned_rows, coarsest)


def solution(mesh):
    placed = (
        P(("sect", "rows"), None, None, None),
        P(("sect", "rows"), None),
        P(("sect", "rows")),
        P(("sect", "rows"), None, None),
        P(("sect", "rows")),
        P(("sect", "rows"), None),
    )
    return jax.shard_map(
        per_device,
        mesh=mesh,
        in_specs=placed,
        out_specs=(P(("sect", "rows"), None), P()),
        check_vma=False,
    )
```

```python
import functools

import jax
import jax.numpy as jnp
from jax import lax
from jax.experimental import pallas as pl
from jax.experimental.pallas import tpu as pltpu
from jax.sharding import PartitionSpec as P

CBS = 16
TILE = 128
RB = 16
KA = 27
AHEAD = 3
CUTS = 3
SIDE = 4
WIDTH = CBS * TILE
C2 = 256

HALF_A = (2, 1)
HALF_B = (3, 0)
FAR = [2 * SIDE + dv for dv in HALF_A + HALF_B]
NEXT_ALONE = [1 * SIDE + dv for dv in HALF_B] + [3 * SIDE + dv for dv in HALF_A]
OWN = [0 * SIDE + dv for dv in HALF_A + HALF_B]
NEXT_JOINED = [1 * SIDE + dv for dv in HALF_A] + [3 * SIDE + dv for dv in HALF_B]
SEQUENCE = FAR + NEXT_ALONE + NEXT_JOINED + OWN
PAIRS = len(SEQUENCE) // 2
COUNT, ORDER, STARTS, INFO = KA, KA + 1, KA + 2, KA + 3
Q_SCALE = 2.0**20


def cost(microseconds):
    return pl.CostEstimate(flops=0, bytes_accessed=int(microseconds * 3.7e6), transcendentals=0)


def plan_body(cols, counts, own_map, info, table):
    def fill(i, _):
        for k in range(KA):
            table[i, k] = cols[i, k] - info[4]
        table[i, COUNT] = counts[i]
        table[i, INFO] = info[lax.min(i, 7)]
        return 0

    lax.fori_loop(0, RB, fill, 0)
    first_core = info[1] == 0
    names = []
    for i in range(RB):
        block = own_map[i] - info[0]
        high, low = lax.shift_right_logical(block, 2), lax.bitwise_and(block, 3)
        du = lax.bitwise_and(jnp.where(first_core, high, low) - info[2], 3)
        dv = lax.bitwise_and(jnp.where(first_core, low, high) - info[3], 3)
        names.append(du * SIDE + dv)
    n = jnp.int32(0)
    for j, code in enumerate(SEQUENCE):
        table[j, STARTS] = n
        for i in range(RB):
            table[n, ORDER] = jnp.int32(i)
            n = n + (names[i] == code).astype(jnp.int32)
    table[len(SEQUENCE), STARTS] = n


def row_plan(*operands):
    smem = pl.BlockSpec(memory_space=pltpu.SMEM)
    return pl.pallas_call(
        plan_body,
        out_shape=jax.ShapeDtypeStruct((RB + 1, 32), jnp.int32),
        in_specs=[smem] * len(operands),
        out_specs=smem,
        cost_estimate=cost(3),
    )(*operands)


def galerkin_body(table, maps, a_ref, left_ref, own_ref, right_ref, *rest):
    outs, (scale_ref, a_buf, tiles, acc, stage, a_sem, p_sem, out_sem) = rest[:PAIRS], rest[PAIRS:]
    scale_ref[...] = jnp.full(scale_ref.shape, 1.0 / Q_SCALE, jnp.float32)

    def fetch(r):
        slot = lax.rem(r, AHEAD + 1)
        part = KA // CUTS
        return [
            pltpu.make_async_copy(
                a_ref.at[table[r, ORDER], pl.ds(n * part, part)], a_buf.at[slot, pl.ds(n * part, part)], a_sem.at[slot, n]
            )
            for n in range(CUTS)
        ]

    for r in range(AHEAD):
        for copy in fetch(r):
            copy.start()
    loads = [
        pltpu.make_async_copy(src.at[pl.ds(0, RB)], tiles.at[pl.ds(n * RB, RB)], p_sem.at[n])
        for n, src in enumerate((left_ref, own_ref, right_ref))
    ]
    for load in loads:
        load.start()
    acc[...] = jnp.zeros_like(acc)
    for load in loads:
        load.wait()

    def row(r, _):
        @pl.when(r + AHEAD < RB)
        def _():
            for copy in fetch(r + AHEAD):
                copy.start()

        for copy in fetch(r):
            copy.wait()
        i = table[r, ORDER]
        slot = lax.rem(r, AHEAD + 1)
        count = table[i, COUNT]
        left = tiles[RB + i].T
        blank = jnp.zeros((TILE, TILE), jnp.bfloat16)
        for k in range(0, KA, 2):
            slots = range(k, min(k + 2, KA))
            rights, places = [], []
            for s in slots:
                col = jnp.clip(table[i, s], 0, 3 * RB - 1)
                block = jnp.clip(maps[lax.shift_right_logical(col, 4), lax.bitwise_and(col, RB - 1)], 0, CBS - 1)
                places.append(pl.multiple_of(jnp.where(s < count, block, CBS) * TILE, TILE))
                rights.append(tiles[col])
            if len(rights) == 2:
                fine = jnp.concatenate([a_buf[slot, s] for s in slots], axis=1)
                coarse = jnp.concatenate([
                    jnp.concatenate([rights[0], blank], axis=1), jnp.concatenate([blank, rights[1]], axis=1)
                ], axis=0)
            else:
                fine, coarse = a_buf[slot, k], rights[0]
            products = jnp.dot(fine, coarse, preferred_element_type=jnp.float32).astype(jnp.bfloat16)
            terms = jnp.dot(left, products, preferred_element_type=jnp.float32)
            for n, place in enumerate(places):
                acc[:, pl.ds(place, TILE)] += terms[:, n * TILE:(n + 1) * TILE]
        return 0

    def leave(n, half):
        return pltpu.make_async_copy(stage.at[half], outs[n].at[half], out_sem.at[half])

    def block(t, _):
        pair, half = lax.div(t, 2), lax.rem(t, 2)
        lax.fori_loop(table[t, STARTS], table[t + 1, STARTS], row, 0)

        @pl.when(pair > 0)
        def _():
            leave(0, half).wait()

        for first in range(0, WIDTH, TILE):
            columns = pl.ds(first, TILE)
            stage[half, :, columns] = acc[:, columns].astype(jnp.bfloat16)
            acc[:, columns] = jnp.zeros((TILE, TILE), jnp.float32)
        for n in range(PAIRS):
            @pl.when(pair == n)
            def _(n=n):
                leave(n, half).start()
        return 0

    lax.fori_loop(0, 2 * PAIRS, block, 0)
    for half in range(2):
        leave(0, half).wait()


def galerkin(table, maps, a_tiles, left, own, right):
    anywhere = pl.BlockSpec(memory_space=pl.ANY)
    return pl.pallas_call(
        galerkin_body,
        out_shape=[jax.ShapeDtypeStruct((2, TILE, WIDTH), jnp.bfloat16)] * PAIRS
        + [jax.ShapeDtypeStruct((1, TILE), jnp.float32)],
        grid_spec=pltpu.PrefetchScalarGridSpec(
            num_scalar_prefetch=2,
            grid=(1,),
            in_specs=[pl.BlockSpec(memory_space=pltpu.HBM)] + [anywhere] * 3,
            out_specs=[anywhere] * PAIRS + [pl.BlockSpec((1, TILE), lambda j, *_: (0, 0))],
            scratch_shapes=[
                pltpu.VMEM((AHEAD + 1, KA, TILE, TILE), jnp.bfloat16),
                pltpu.VMEM((3 * RB, TILE, TILE), jnp.bfloat16),
                pltpu.VMEM((TILE, WIDTH + TILE), jnp.float32),
                pltpu.VMEM((2, TILE, WIDTH), jnp.bfloat16),
                pltpu.SemaphoreType.DMA((AHEAD + 1, CUTS)),
                pltpu.SemaphoreType.DMA((3,)),
                pltpu.SemaphoreType.DMA((2,)),
            ],
        ),
        compiler_params=pltpu.CompilerParams(vmem_limit_bytes=52 * 1024 * 1024),
        cost_estimate=cost(20),
    )(table, maps, a_tiles, left, own, right)


def coarsest_body(table, *refs):
    parts = refs[:PAIRS]
    high_ref, low_ref, out_ref, right, rest, left, left_rest, applied, applied_rest, held, q_sem, part_sem = refs[PAIRS:]

    def block_at(u, v):
        u, v = lax.bitwise_and(table[2, INFO] + u, 3), lax.bitwise_and(table[3, INFO] + v, 3)
        block = jnp.where(table[1, INFO] == 0, u * SIDE + v, v * SIDE + u)
        return pl.ds(pl.multiple_of(block * TILE, TILE), TILE)

    factors = [
        pltpu.make_async_copy(src.at[n], dst.at[block_at(n % SIDE, n // SIDE)], q_sem.at[m])
        for m, (src, dst) in enumerate(((high_ref, right), (low_ref, rest)))
        for n in range(CBS)
    ]
    loads = [
        pltpu.make_async_copy(part, held.at[pl.ds(2 * n, 2)], part_sem.at[n]) for n, part in enumerate(parts)
    ]
    for copy in factors[:CBS] + loads[:4] + factors[CBS:]:
        copy.start()
    for m, (src, dst) in enumerate(((high_ref, right), (low_ref, rest))):
        pltpu.make_async_copy(src, dst.reshape(CBS, TILE, C2), q_sem.at[m]).wait()
    for n, code in enumerate(SEQUENCE):
        place, columns = block_at(code // SIDE, code % SIDE), pl.ds(n * TILE, TILE)
        left[:, columns] = right[place, :].T
        left_rest[:, columns] = rest[place, :].T
    for n in range(PAIRS):
        loads[n].wait()
        if n + 4 < PAIRS:
            loads[n + 4].start()
        for m in (2 * n, 2 * n + 1):
            value = jnp.dot(held[m], right[...], preferred_element_type=jnp.float32)
            high = value.astype(jnp.bfloat16)
            rows = pl.ds(m * TILE, TILE)
            applied[rows, :] = high
            applied_rest[rows, :] = (value - high.astype(jnp.float32)).astype(jnp.bfloat16)
    for first in range(0, C2, TILE):
        rows = pl.ds(first, TILE)
        term = jnp.dot(left[rows, :], applied[...], preferred_element_type=jnp.float32)
        term += jnp.dot(left[rows, :], applied_rest[...], preferred_element_type=jnp.float32)
        term += jnp.dot(left_rest[rows, :], applied[...], preferred_element_type=jnp.float32)
        out_ref[rows, :] = term


def coarsest_term(table, parts, high, low):
    return pl.pallas_call(
        coarsest_body,
        out_shape=jax.ShapeDtypeStruct((C2, C2), jnp.float32),
        grid_spec=pltpu.PrefetchScalarGridSpec(
            num_scalar_prefetch=1,
            grid=(1,),
            in_specs=[pl.BlockSpec(memory_space=pl.ANY)] * (PAIRS + 2),
            out_specs=pl.BlockSpec((C2, C2), lambda j, *_: (0, 0)),
            scratch_shapes=[
                pltpu.VMEM((WIDTH, C2), jnp.bfloat16),
                pltpu.VMEM((WIDTH, C2), jnp.bfloat16),
                pltpu.VMEM((C2, WIDTH), jnp.bfloat16),
                pltpu.VMEM((C2, WIDTH), jnp.bfloat16),
                pltpu.VMEM((WIDTH, C2), jnp.bfloat16),
                pltpu.VMEM((WIDTH, C2), jnp.bfloat16),
                pltpu.VMEM((2 * PAIRS, TILE, WIDTH), jnp.bfloat16),
                pltpu.SemaphoreType.DMA((2,)),
                pltpu.SemaphoreType.DMA((PAIRS,)),
            ],
        ),
        compiler_params=pltpu.CompilerParams(vmem_limit_bytes=52 * 1024 * 1024),
        cost_estimate=cost(6),
    )(table, *parts, high, low)


def held_back(value, after_this):
    anywhere = pl.BlockSpec(memory_space=pl.ANY)
    return pl.pallas_call(
        lambda *refs: None,
        out_shape=jax.ShapeDtypeStruct(value.shape, value.dtype),
        in_specs=[anywhere] * 2,
        out_specs=anywhere,
        input_output_aliases={0: 0},
        cost_estimate=cost(1),
    )(value, after_this)


def joined_body(up, from_far_a, down, from_far_b, _, up_out, down_out):
    up_out[...] = (up[...].astype(jnp.float32) + from_far_a[...].astype(jnp.float32)).astype(jnp.bfloat16)
    down_out[...] = (down[...].astype(jnp.float32) + from_far_b[...].astype(jnp.float32)).astype(jnp.bfloat16)


def joined(up, from_far_a, down, from_far_b, after_this):
    rows = 32
    part = pl.BlockSpec((2, rows, WIDTH), lambda j: (0, j, 0))
    return pl.pallas_call(
        joined_body,
        out_shape=[jax.ShapeDtypeStruct(up.shape, jnp.bfloat16)] * 2,
        grid=(TILE // rows,),
        in_specs=[part] * 4 + [pl.BlockSpec(memory_space=pl.ANY)],
        out_specs=[part] * 2,
        compiler_params=pltpu.CompilerParams(vmem_limit_bytes=32 * 1024 * 1024),
        cost_estimate=cost(2),
    )(up, from_far_a, down, from_far_b, after_this)


def torus_steps():
    def pairs(second, target):
        found = []
        for sect in range(8):
            for row in range(SIDE * SIDE):
                at = [row // SIDE, row % SIDE]
                axis = (sect % 2) ^ second
                at[axis] = target(at[axis])
                found.append((sect * 16 + row, sect * 16 + at[0] * SIDE + at[1]))
        return found

    return [{by: pairs(second, lambda at: (at + by) % SIDE) for by in (1, -1, 2)} for second in (0, 1)]


STEPS = torus_steps()


def send(value, second, by):
    return lax.ppermute(value, ("sect", "rows"), STEPS[second][by])


def wide(value):
    return value.astype(jnp.float32)


def share_out(term):
    pieces = term.reshape(32, 8, 2, 128).transpose(0, 2, 1, 3).reshape(128, 4, 128)
    return jnp.sum(lax.all_to_all(pieces, ("sect", "rows"), 0, 0), axis=0)


def bring_back(piece):
    back = lax.all_to_all(jnp.broadcast_to(piece[None], (128,) + piece.shape), ("sect", "rows"), 0, 0)
    return back.reshape(32, 2, 8, 128).transpose(0, 2, 1, 3).reshape(C2, C2)


def around(value, second):
    return jnp.stack([value, send(value, second, -1), send(value, second, 2), send(value, second, 1)])


def reduced_body(own_a, own_b, up_a, up_b, down_a, down_b, _, far, after, before, mine):
    def total(n, *refs):
        value = refs[0][n].astype(jnp.float32)
        for ref in refs[1:]:
            value = value + ref[n].astype(jnp.float32)
        return value

    far[...] = total(0, own_a, up_a, down_a).astype(jnp.bfloat16)
    after[...] = total(1, own_a, up_a, down_a).astype(jnp.bfloat16)
    before[...] = total(0, own_b, up_b, down_b).astype(jnp.bfloat16)
    mine[...] = total(1, own_b, up_b, down_b)


def reduced(own_a, own_b, up_a, up_b, down_a, down_b, after_this):
    rows = 64
    pair = pl.BlockSpec((2, rows, WIDTH), lambda j: (0, j, 0))
    one = pl.BlockSpec((rows, WIDTH), lambda j: (j, 0))
    shape = (TILE, WIDTH)
    return pl.pallas_call(
        reduced_body,
        out_shape=[jax.ShapeDtypeStruct(shape, jnp.bfloat16)] * 3 + [jax.ShapeDtypeStruct(shape, jnp.float32)],
        grid=(TILE // rows,),
        in_specs=[pair] * 6 + [pl.BlockSpec(memory_space=pl.ANY)],
        out_specs=[one] * 4,
        compiler_params=pltpu.CompilerParams(vmem_limit_bytes=32 * 1024 * 1024),
        cost_estimate=cost(3),
    )(own_a, own_b, up_a, up_b, down_a, down_b, after_this)


def per_device(a_tiles, a_cols, a_count, p_tiles, coarse_map, p_coarse):
    section = lax.axis_index("sect")
    position = lax.axis_index("rows")
    core = lax.rem(section, 2)
    x, y = lax.div(position, SIDE), lax.rem(position, SIDE)
    u, v = jnp.where(core == 0, x, y), jnp.where(core == 0, y, x)
    zero = jnp.zeros_like(core)
    first_row = (section * 16 + position - 1) * RB
    info = jnp.stack([section * CBS, core, u, v, first_row, zero, zero, zero]).astype(jnp.int32)
    up = [(i, i + 1) for i in range(15)]
    down = [(i + 1, i) for i in range(15)]
    local_map = coarse_map - section * CBS
    map_tile = jnp.pad(local_map.astype(jnp.bfloat16)[None, None], ((0, 0), (0, TILE - 1), (0, TILE - RB)))
    own = jnp.concatenate([p_tiles, map_tile], axis=0)
    left, right = lax.ppermute(own, "rows", up), lax.ppermute(own, "rows", down)
    maps = jnp.stack([left[RB, 0, :RB].astype(jnp.int32), local_map, right[RB, 0, :RB].astype(jnp.int32)])

    line = around((p_coarse * Q_SCALE).astype(jnp.float16), 0)
    square = around(line, 1)
    table = row_plan(a_cols, a_count, coarse_map, info)
    *parts, scale = galerkin(table, maps, a_tiles, left, own, right)
    far_a, far_b, up_b, down_a, up_a, down_b, own_a, own_b = parts
    prolong = square.reshape(CBS, TILE, C2).astype(jnp.float32) * scale[0, 0]
    prolong_high = lax.reduce_precision(prolong, 8, 7)
    prolong_low = (prolong - prolong_high).astype(jnp.bfloat16)
    prolong_high = prolong_high.astype(jnp.bfloat16)
    far_a = held_back(far_a, prolong_high)
    parts = (far_a, far_b, up_b, down_a, up_a, down_b, own_a, own_b)
    from_far_a, from_far_b = send(far_a, 0, 1), send(far_b, 0, -1)
    from_up_b, from_down_a = send(up_b, 0, 1), send(down_a, 0, -1)
    own_term = coarsest_term(table, parts, prolong_high, prolong_low)
    up_a, down_b = joined(up_a, from_far_a, down_b, from_far_b, own_term)
    from_up_a, from_down_b = send(up_a, 0, 1), send(down_b, 0, -1)

    own_piece = share_out(own_term)
    far, after, before, mine = reduced(own_a, own_b, from_up_a, from_up_b, from_down_a, from_down_b, own_piece)
    from_far, from_after, from_before = send(far, 1, 2), send(after, 1, 1), send(before, 1, -1)
    coarsest = bring_back(own_piece)
    owned_rows = mine + (wide(from_far) + (wide(from_after) + wide(from_before)))
    return (owned_rows, coarsest)


def solution(mesh):
    placed = (
        P(("sect", "rows"), None, None, None),
        P(("sect", "rows"), None),
        P(("sect", "rows")),
        P(("sect", "rows"), None, None),
        P(("sect", "rows")),
        P(("sect", "rows"), None),
    )
    return jax.shard_map(
        per_device,
        mesh=mesh,
        in_specs=placed,
        out_specs=(P(("sect", "rows"), None), P()),
        check_vma=False,
    )
```

```python
import functools

import jax
import jax.numpy as jnp
from jax import lax
from jax.experimental import pallas as pl
from jax.experimental.pallas import tpu as pltpu
from jax.sharding import PartitionSpec as P

CBS = 16
TILE = 128
RB = 16
KA = 27
GROUP = 2
AHEAD = 3
CUTS = 3
STAGES = 4
SIDE = 4
WIDTH = CBS * TILE
C2 = 256

HALF_A = (2, 1)
HALF_B = (3, 0)
FAR = [2 * SIDE + dv for dv in HALF_A + HALF_B]
NEXT_ALONE = [1 * SIDE + dv for dv in HALF_B] + [3 * SIDE + dv for dv in HALF_A]
OWN = [0 * SIDE + dv for dv in HALF_A + HALF_B]
NEXT_JOINED = [1 * SIDE + dv for dv in HALF_A] + [3 * SIDE + dv for dv in HALF_B]
SEQUENCE = FAR + NEXT_ALONE + NEXT_JOINED + OWN
PAIRS = len(SEQUENCE) // 2
COUNT, ORDER, STARTS, INFO = KA, KA + 1, KA + 2, KA + 3
Q_SCALE = 2.0**20


def cost(microseconds):
    return pl.CostEstimate(flops=0, bytes_accessed=int(microseconds * 3.7e6), transcendentals=0)


def plan_body(cols, counts, own_map, info, table):
    def fill(i, _):
        for k in range(KA):
            table[i, k] = cols[i, k] - info[4]
        table[i, COUNT] = counts[i]
        table[i, INFO] = info[lax.min(i, 7)]
        return 0

    lax.fori_loop(0, RB, fill, 0)
    first_core = info[1] == 0
    names = []
    for i in range(RB):
        block = own_map[i] - info[0]
        high, low = lax.shift_right_logical(block, 2), lax.bitwise_and(block, 3)
        du = lax.bitwise_and(jnp.where(first_core, high, low) - info[2], 3)
        dv = lax.bitwise_and(jnp.where(first_core, low, high) - info[3], 3)
        names.append(du * SIDE + dv)
    n = jnp.int32(0)
    for j, code in enumerate(SEQUENCE):
        table[j, STARTS] = n
        for i in range(RB):
            table[n, ORDER] = jnp.int32(i)
            n = n + (names[i] == code).astype(jnp.int32)
    table[len(SEQUENCE), STARTS] = n


def row_plan(*operands):
    smem = pl.BlockSpec(memory_space=pltpu.SMEM)
    return pl.pallas_call(
        plan_body,
        out_shape=jax.ShapeDtypeStruct((RB + 1, 32), jnp.int32),
        in_specs=[smem] * len(operands),
        out_specs=smem,
        cost_estimate=cost(3),
    )(*operands)


def galerkin_body(table, maps, a_ref, left_ref, own_ref, right_ref, *rest):
    outs, (scale_ref, a_buf, tiles, acc, stage, a_sem, p_sem, out_sem) = rest[:PAIRS], rest[PAIRS:]
    scale_ref[...] = jnp.full(scale_ref.shape, 1.0 / Q_SCALE, jnp.float32)

    def fetch(r):
        slot = lax.rem(r, AHEAD + 1)
        part = KA // CUTS
        return [
            pltpu.make_async_copy(
                a_ref.at[table[r, ORDER], pl.ds(n * part, part)], a_buf.at[slot, pl.ds(n * part, part)], a_sem.at[slot, n]
            )
            for n in range(CUTS)
        ]

    loads = [
        pltpu.make_async_copy(src.at[pl.ds(0, RB)], tiles.at[pl.ds(n * RB, RB)], p_sem.at[n])
        for n, src in enumerate((left_ref, own_ref, right_ref))
    ]
    for load in loads:
        load.start()
    for r in range(AHEAD):
        for copy in fetch(r):
            copy.start()
    acc[...] = jnp.zeros_like(acc)
    for load in loads:
        load.wait()

    def row(r, _):
        @pl.when(r + AHEAD < RB)
        def _():
            for copy in fetch(r + AHEAD):
                copy.start()

        for copy in fetch(r):
            copy.wait()
        i = table[r, ORDER]
        slot = lax.rem(r, AHEAD + 1)
        count = table[i, COUNT]
        left = tiles[RB + i].T
        for k in range(0, KA, GROUP):
            products, places = [], []
            for s in range(k, min(k + GROUP, KA)):
                col = jnp.clip(table[i, s], 0, 3 * RB - 1)
                block = jnp.clip(maps[lax.shift_right_logical(col, 4), lax.bitwise_and(col, RB - 1)], 0, CBS - 1)
                places.append(pl.multiple_of(jnp.where(s < count, block, CBS) * TILE, TILE))
                products.append(
                    jnp.dot(a_buf[slot, s], tiles[col], preferred_element_type=jnp.float32).astype(jnp.bfloat16)
                )
            terms = jnp.dot(left, jnp.concatenate(products, axis=1) if len(products) > 1 else products[0], preferred_element_type=jnp.float32)
            for n, place in enumerate(places):
                acc[:, pl.ds(place, TILE)] += terms[:, n * TILE:(n + 1) * TILE]
        return 0

    def leave(n, half, slot):
        return pltpu.make_async_copy(stage.at[slot], outs[n].at[half], out_sem.at[slot])

    def block(t, _):
        pair, half, slot = lax.div(t, 2), lax.rem(t, 2), lax.rem(t, STAGES)
        lax.fori_loop(table[t, STARTS], table[t + 1, STARTS], row, 0)

        @pl.when(t >= STAGES)
        def _():
            leave(0, 0, slot).wait()

        for first in range(0, WIDTH, TILE):
            columns = pl.ds(first, TILE)
            stage[slot, :, columns] = acc[:, columns].astype(jnp.bfloat16)
            acc[:, columns] = jnp.zeros((TILE, TILE), jnp.float32)
        for n in range(PAIRS):
            @pl.when(pair == n)
            def _(n=n):
                leave(n, half, slot).start()
        return 0

    lax.fori_loop(0, 2 * PAIRS, block, 0)
    for slot in range(STAGES):
        leave(0, 0, slot).wait()


def galerkin(table, maps, a_tiles, left, own, right):
    anywhere = pl.BlockSpec(memory_space=pl.ANY)
    return pl.pallas_call(
        galerkin_body,
        out_shape=[jax.ShapeDtypeStruct((2, TILE, WIDTH), jnp.bfloat16)] * PAIRS
        + [jax.ShapeDtypeStruct((1, TILE), jnp.float32)],
        grid_spec=pltpu.PrefetchScalarGridSpec(
            num_scalar_prefetch=2,
            grid=(1,),
            in_specs=[pl.BlockSpec(memory_space=pltpu.HBM)] + [anywhere] * 3,
            out_specs=[anywhere] * PAIRS + [pl.BlockSpec((1, TILE), lambda j, *_: (0, 0))],
            scratch_shapes=[
                pltpu.VMEM((AHEAD + 1, KA, TILE, TILE), jnp.bfloat16),
                pltpu.VMEM((3 * RB, TILE, TILE), jnp.bfloat16),
                pltpu.VMEM((TILE, WIDTH + TILE), jnp.float32),
                pltpu.VMEM((STAGES, TILE, WIDTH), jnp.bfloat16),
                pltpu.SemaphoreType.DMA((AHEAD + 1, CUTS)),
                pltpu.SemaphoreType.DMA((3,)),
                pltpu.SemaphoreType.DMA((STAGES,)),
            ],
        ),
        compiler_params=pltpu.CompilerParams(vmem_limit_bytes=52 * 1024 * 1024),
        cost_estimate=cost(20),
    )(table, maps, a_tiles, left, own, right)


def coarsest_body(table, *refs):
    parts = refs[:PAIRS]
    high_ref, low_ref, out_ref, right, rest, left, left_rest, applied, applied_rest, held, q_sem, part_sem = refs[PAIRS:]

    def block_at(u, v):
        u, v = lax.bitwise_and(table[2, INFO] + u, 3), lax.bitwise_and(table[3, INFO] + v, 3)
        block = jnp.where(table[1, INFO] == 0, u * SIDE + v, v * SIDE + u)
        return pl.ds(pl.multiple_of(block * TILE, TILE), TILE)

    factors = [
        pltpu.make_async_copy(src.at[n], dst.at[block_at(n % SIDE, n // SIDE)], q_sem.at[m])
        for m, (src, dst) in enumerate(((high_ref, right), (low_ref, rest)))
        for n in range(CBS)
    ]
    loads = [
        pltpu.make_async_copy(part, held.at[pl.ds(2 * n, 2)], part_sem.at[n]) for n, part in enumerate(parts)
    ]
    for copy in factors[:CBS] + loads[:4] + factors[CBS:]:
        copy.start()
    for m, (src, dst) in enumerate(((high_ref, right), (low_ref, rest))):
        pltpu.make_async_copy(src, dst.reshape(CBS, TILE, C2), q_sem.at[m]).wait()
    for n, code in enumerate(SEQUENCE):
        place, columns = block_at(code // SIDE, code % SIDE), pl.ds(n * TILE, TILE)
        left[:, columns] = right[place, :].T
        left_rest[:, columns] = rest[place, :].T
    for n in range(PAIRS):
        loads[n].wait()
        if n + 4 < PAIRS:
            loads[n + 4].start()
        for m in (2 * n, 2 * n + 1):
            value = jnp.dot(held[m], right[...], preferred_element_type=jnp.float32)
            high = value.astype(jnp.bfloat16)
            rows = pl.ds(m * TILE, TILE)
            applied[rows, :] = high
            applied_rest[rows, :] = (value - high.astype(jnp.float32)).astype(jnp.bfloat16)
    for first in range(0, C2, TILE):
        rows = pl.ds(first, TILE)
        term = jnp.dot(left[rows, :], applied[...], preferred_element_type=jnp.float32)
        term += jnp.dot(left[rows, :], applied_rest[...], preferred_element_type=jnp.float32)
        term += jnp.dot(left_rest[rows, :], applied[...], preferred_element_type=jnp.float32)
        out_ref[rows, :] = term


def coarsest_term(table, parts, high, low):
    return pl.pallas_call(
        coarsest_body,
        out_shape=jax.ShapeDtypeStruct((C2, C2), jnp.float32),
        grid_spec=pltpu.PrefetchScalarGridSpec(
            num_scalar_prefetch=1,
            grid=(1,),
            in_specs=[pl.BlockSpec(memory_space=pl.ANY)] * (PAIRS + 2),
            out_specs=pl.BlockSpec((C2, C2), lambda j, *_: (0, 0)),
            scratch_shapes=[
                pltpu.VMEM((WIDTH, C2), jnp.bfloat16),
                pltpu.VMEM((WIDTH, C2), jnp.bfloat16),
                pltpu.VMEM((C2, WIDTH), jnp.bfloat16),
                pltpu.VMEM((C2, WIDTH), jnp.bfloat16),
                pltpu.VMEM((WIDTH, C2), jnp.bfloat16),
                pltpu.VMEM((WIDTH, C2), jnp.bfloat16),
                pltpu.VMEM((2 * PAIRS, TILE, WIDTH), jnp.bfloat16),
                pltpu.SemaphoreType.DMA((2,)),
                pltpu.SemaphoreType.DMA((PAIRS,)),
            ],
        ),
        compiler_params=pltpu.CompilerParams(vmem_limit_bytes=52 * 1024 * 1024),
        cost_estimate=cost(6),
    )(table, *parts, high, low)


def held_back(first, second, after_this):
    anywhere = pl.BlockSpec(memory_space=pl.ANY)
    return pl.pallas_call(
        lambda *refs: None,
        out_shape=[jax.ShapeDtypeStruct(value.shape, value.dtype) for value in (first, second)],
        in_specs=[anywhere] * 3,
        out_specs=[anywhere] * 2,
        input_output_aliases={0: 0, 1: 1},
        cost_estimate=cost(1),
    )(first, second, after_this)


def joined_body(up, from_far_a, down, from_far_b, _, up_out, down_out):
    up_out[...] = (up[...].astype(jnp.float32) + from_far_a[...].astype(jnp.float32)).astype(jnp.bfloat16)
    down_out[...] = (down[...].astype(jnp.float32) + from_far_b[...].astype(jnp.float32)).astype(jnp.bfloat16)


def joined(up, from_far_a, down, from_far_b, after_this):
    rows = 32
    part = pl.BlockSpec((2, rows, WIDTH), lambda j: (0, j, 0))
    return pl.pallas_call(
        joined_body,
        out_shape=[jax.ShapeDtypeStruct(up.shape, jnp.bfloat16)] * 2,
        grid=(TILE // rows,),
        in_specs=[part] * 4 + [pl.BlockSpec(memory_space=pl.ANY)],
        out_specs=[part] * 2,
        compiler_params=pltpu.CompilerParams(vmem_limit_bytes=32 * 1024 * 1024),
        cost_estimate=cost(2),
    )(up, from_far_a, down, from_far_b, after_this)


def torus_steps():
    def pairs(second, target):
        found = []
        for sect in range(8):
            for row in range(SIDE * SIDE):
                at = [row // SIDE, row % SIDE]
                axis = (sect % 2) ^ second
                at[axis] = target(at[axis])
                found.append((sect * 16 + row, sect * 16 + at[0] * SIDE + at[1]))
        return found

    return [{by: pairs(second, lambda at: (at + by) % SIDE) for by in (1, -1, 2)} for second in (0, 1)]


STEPS = torus_steps()


def send(value, second, by):
    return lax.ppermute(value, ("sect", "rows"), STEPS[second][by])


def wide(value):
    return value.astype(jnp.float32)


def share_out(term):
    pieces = term.reshape(32, 8, 2, 128).transpose(0, 2, 1, 3).reshape(128, 4, 128)
    return jnp.sum(lax.all_to_all(pieces, ("sect", "rows"), 0, 0), axis=0)


def bring_back(piece):
    back = lax.all_to_all(jnp.broadcast_to(piece[None], (128,) + piece.shape), ("sect", "rows"), 0, 0)
    return back.reshape(32, 2, 8, 128).transpose(0, 2, 1, 3).reshape(C2, C2)


def around(value, second):
    return jnp.stack([value, send(value, second, -1), send(value, second, 2), send(value, second, 1)])


def reduced_body(own_a, own_b, up_a, up_b, down_a, down_b, _, far, after, before, mine):
    def total(n, *refs):
        value = refs[0][n].astype(jnp.float32)
        for ref in refs[1:]:
            value = value + ref[n].astype(jnp.float32)
        return value

    far[...] = total(0, own_a, up_a, down_a).astype(jnp.bfloat16)
    after[...] = total(1, own_a, up_a, down_a).astype(jnp.bfloat16)
    before[...] = total(0, own_b, up_b, down_b).astype(jnp.bfloat16)
    mine[...] = total(1, own_b, up_b, down_b)


def reduced(own_a, own_b, up_a, up_b, down_a, down_b, after_this):
    rows = 64
    pair = pl.BlockSpec((2, rows, WIDTH), lambda j: (0, j, 0))
    one = pl.BlockSpec((rows, WIDTH), lambda j: (j, 0))
    shape = (TILE, WIDTH)
    return pl.pallas_call(
        reduced_body,
        out_shape=[jax.ShapeDtypeStruct(shape, jnp.bfloat16)] * 3 + [jax.ShapeDtypeStruct(shape, jnp.float32)],
        grid=(TILE // rows,),
        in_specs=[pair] * 6 + [pl.BlockSpec(memory_space=pl.ANY)],
        out_specs=[one] * 4,
        compiler_params=pltpu.CompilerParams(vmem_limit_bytes=32 * 1024 * 1024),
        cost_estimate=cost(3),
    )(own_a, own_b, up_a, up_b, down_a, down_b, after_this)


def per_device(a_tiles, a_cols, a_count, p_tiles, coarse_map, p_coarse):
    section = lax.axis_index("sect")
    position = lax.axis_index("rows")
    core = lax.rem(section, 2)
    x, y = lax.div(position, SIDE), lax.rem(position, SIDE)
    u, v = jnp.where(core == 0, x, y), jnp.where(core == 0, y, x)
    zero = jnp.zeros_like(core)
    first_row = (section * 16 + position - 1) * RB
    info = jnp.stack([section * CBS, core, u, v, first_row, zero, zero, zero]).astype(jnp.int32)
    up = [(i, i + 1) for i in range(15)]
    down = [(i + 1, i) for i in range(15)]
    local_map = coarse_map - section * CBS
    map_tile = jnp.pad(local_map.astype(jnp.bfloat16)[None, None], ((0, 0), (0, TILE - 1), (0, TILE - RB)))
    own = jnp.concatenate([p_tiles, map_tile], axis=0)
    left, right = lax.ppermute(own, "rows", up), lax.ppermute(own, "rows", down)
    maps = jnp.stack([left[RB, 0, :RB].astype(jnp.int32), local_map, right[RB, 0, :RB].astype(jnp.int32)])

    line = around((p_coarse * Q_SCALE).astype(jnp.float16), 0)
    square = around(line, 1)
    table = row_plan(a_cols, a_count, coarse_map, info)
    *parts, scale = galerkin(table, maps, a_tiles, left, own, right)
    far_a, far_b, up_b, down_a, up_a, down_b, own_a, own_b = parts
    prolong = square.reshape(CBS, TILE, C2).astype(jnp.float32) * scale[0, 0]
    prolong_high = lax.reduce_precision(prolong, 8, 7)
    prolong_low = (prolong - prolong_high).astype(jnp.bfloat16)
    prolong_high = prolong_high.astype(jnp.bfloat16)
    square_held = jnp.sum(square[1:, 0, :8, :TILE].astype(jnp.float32) * scale, axis=0)
    far_a, far_b = held_back(far_a, far_b, square_held)
    parts = (far_a, far_b, up_b, down_a, up_a, down_b, own_a, own_b)
    from_far_a, from_far_b = send(far_a, 0, 1), send(far_b, 0, -1)
    from_up_b, from_down_a = send(up_b, 0, 1), send(down_a, 0, -1)
    own_term = coarsest_term(table, parts, prolong_high, prolong_low)
    up_a, down_b = joined(up_a, from_far_a, down_b, from_far_b, own_term)
    from_up_a, from_down_b = send(up_a, 0, 1), send(down_b, 0, -1)

    own_piece = share_out(own_term)
    far, after, before, mine = reduced(own_a, own_b, from_up_a, from_up_b, from_down_a, from_down_b, own_piece)
    from_far, from_after, from_before = send(far, 1, 2), send(after, 1, 1), send(before, 1, -1)
    coarsest = bring_back(own_piece)
    owned_rows = mine + (wide(from_far) + (wide(from_after) + wide(from_before)))
    return (owned_rows, coarsest)


def solution(mesh):
    placed = (
        P(("sect", "rows"), None, None, None),
        P(("sect", "rows"), None),
        P(("sect", "rows")),
        P(("sect", "rows"), None, None),
        P(("sect", "rows")),
        P(("sect", "rows"), None),
    )
    return jax.shard_map(
        per_device,
        mesh=mesh,
        in_specs=placed,
        out_specs=(P(("sect", "rows"), None), P()),
        check_vma=False,
    )
```

```python
import functools

import jax
import jax.numpy as jnp
from jax import lax
from jax.experimental import pallas as pl
from jax.experimental.pallas import tpu as pltpu
from jax.sharding import PartitionSpec as P

CBS = 16
TILE = 128
RB = 16
KA = 27
GROUP = 2
AHEAD = 3
CUTS = 3
STAGES = 4
SIDE = 4
WIDTH = CBS * TILE
C2 = 256

HALF_A = (2, 1)
HALF_B = (3, 0)
FAR = [2 * SIDE + dv for dv in HALF_A + HALF_B]
NEXT_ALONE = [1 * SIDE + dv for dv in HALF_B] + [3 * SIDE + dv for dv in HALF_A]
OWN = [0 * SIDE + dv for dv in HALF_A + HALF_B]
NEXT_JOINED = [1 * SIDE + dv for dv in HALF_A] + [3 * SIDE + dv for dv in HALF_B]
SEQUENCE = FAR + NEXT_ALONE + NEXT_JOINED + OWN
PAIRS = len(SEQUENCE) // 2
COUNT, ORDER, STARTS, INFO = KA, KA + 1, KA + 2, KA + 3
MAPS = RB + 1
Q_SCALE = 2.0**20


def cost(microseconds):
    return pl.CostEstimate(flops=0, bytes_accessed=int(microseconds * 3.7e6), transcendentals=0)


def plan_body(cols, counts, own_map, info, table):
    def fill(i, _):
        for k in range(KA):
            table[i, k] = cols[i, k] - info[4]
        table[i, COUNT] = counts[i]
        table[i, INFO] = info[lax.min(i, 7)]
        return 0

    lax.fori_loop(0, RB, fill, 0)
    first_core = info[1] == 0
    names = []
    for i in range(RB):
        block = own_map[i] - info[0]
        high, low = lax.shift_right_logical(block, 2), lax.bitwise_and(block, 3)
        du = lax.bitwise_and(jnp.where(first_core, high, low) - info[2], 3)
        dv = lax.bitwise_and(jnp.where(first_core, low, high) - info[3], 3)
        names.append(du * SIDE + dv)
    n = jnp.int32(0)
    for j, code in enumerate(SEQUENCE):
        table[j, STARTS] = n
        for i in range(RB):
            table[n, ORDER] = jnp.int32(i)
            n = n + (names[i] == code).astype(jnp.int32)
    table[len(SEQUENCE), STARTS] = n


def row_plan(*operands):
    smem = pl.BlockSpec(memory_space=pltpu.SMEM)
    return pl.pallas_call(
        plan_body,
        out_shape=jax.ShapeDtypeStruct((RB + 1, 32), jnp.int32),
        in_specs=[smem] * len(operands),
        out_specs=smem,
        cost_estimate=cost(3),
    )(*operands)


def galerkin_body(table, a_ref, left_ref, own_ref, right_ref, *rest):
    outs, (scale_ref, a_buf, tiles, acc, stage, a_sem, p_sem, out_sem) = rest[:PAIRS], rest[PAIRS:]
    scale_ref[...] = jnp.full(scale_ref.shape, 1.0 / Q_SCALE, jnp.float32)

    def fetch(r):
        slot = lax.rem(r, AHEAD + 1)
        part = KA // CUTS
        return [
            pltpu.make_async_copy(
                a_ref.at[table[r, ORDER], pl.ds(n * part, part)], a_buf.at[slot, pl.ds(n * part, part)], a_sem.at[slot, n]
            )
            for n in range(CUTS)
        ]

    loads = [
        pltpu.make_async_copy(src.at[pl.ds(0, RB)], tiles.at[pl.ds(n * RB, RB)], p_sem.at[n])
        for n, src in enumerate((left_ref, own_ref, right_ref))
    ]
    for load in loads:
        load.start()
    for r in range(AHEAD):
        for copy in fetch(r):
            copy.start()
    acc[...] = jnp.zeros_like(acc)
    for load in loads:
        load.wait()

    def row(r, _):
        @pl.when(r + AHEAD < RB)
        def _():
            for copy in fetch(r + AHEAD):
                copy.start()

        for copy in fetch(r):
            copy.wait()
        i = table[r, ORDER]
        slot = lax.rem(r, AHEAD + 1)
        count = table[i, COUNT]
        left = tiles[RB + i].T
        for k in range(0, KA, GROUP):
            products, places = [], []
            for s in range(k, min(k + GROUP, KA)):
                col = jnp.clip(table[i, s], 0, 3 * RB - 1)
                block = jnp.clip(table[MAPS + lax.shift_right_logical(col, 4), lax.bitwise_and(col, RB - 1)], 0, CBS - 1)
                places.append(pl.multiple_of(jnp.where(s < count, block, CBS) * TILE, TILE))
                products.append(
                    jnp.dot(a_buf[slot, s], tiles[col], preferred_element_type=jnp.float32).astype(jnp.bfloat16)
                )
            terms = jnp.dot(left, jnp.concatenate(products, axis=1) if len(products) > 1 else products[0], preferred_element_type=jnp.float32)
            for n, place in enumerate(places):
                acc[:, pl.ds(place, TILE)] += terms[:, n * TILE:(n + 1) * TILE]
        return 0

    def leave(n, half, slot):
        return pltpu.make_async_copy(stage.at[slot], outs[n].at[half], out_sem.at[slot])

    def block(t, _):
        pair, half, slot = lax.div(t, 2), lax.rem(t, 2), lax.rem(t, STAGES)
        lax.fori_loop(table[t, STARTS], table[t + 1, STARTS], row, 0)

        @pl.when(t >= STAGES)
        def _():
            leave(0, 0, slot).wait()

        for first in range(0, WIDTH, TILE):
            columns = pl.ds(first, TILE)
            stage[slot, :, columns] = acc[:, columns].astype(jnp.bfloat16)
            acc[:, columns] = jnp.zeros((TILE, TILE), jnp.float32)
        for n in range(PAIRS):
            @pl.when(pair == n)
            def _(n=n):
                leave(n, half, slot).start()
        return 0

    lax.fori_loop(0, 2 * PAIRS, block, 0)
    for slot in range(STAGES):
        leave(0, 0, slot).wait()


def galerkin(table, a_tiles, left, own, right):
    anywhere = pl.BlockSpec(memory_space=pl.ANY)
    return pl.pallas_call(
        galerkin_body,
        out_shape=[jax.ShapeDtypeStruct((2, TILE, WIDTH), jnp.bfloat16)] * PAIRS
        + [jax.ShapeDtypeStruct((1, TILE), jnp.float32)],
        grid_spec=pltpu.PrefetchScalarGridSpec(
            num_scalar_prefetch=1,
            grid=(1,),
            in_specs=[pl.BlockSpec(memory_space=pltpu.HBM)] + [anywhere] * 3,
            out_specs=[anywhere] * PAIRS + [pl.BlockSpec((1, TILE), lambda j, *_: (0, 0))],
            scratch_shapes=[
                pltpu.VMEM((AHEAD + 1, KA, TILE, TILE), jnp.bfloat16),
                pltpu.VMEM((3 * RB, TILE, TILE), jnp.bfloat16),
                pltpu.VMEM((TILE, WIDTH + TILE), jnp.float32),
                pltpu.VMEM((STAGES, TILE, WIDTH), jnp.bfloat16),
                pltpu.SemaphoreType.DMA((AHEAD + 1, CUTS)),
                pltpu.SemaphoreType.DMA((3,)),
                pltpu.SemaphoreType.DMA((STAGES,)),
            ],
        ),
        compiler_params=pltpu.CompilerParams(vmem_limit_bytes=52 * 1024 * 1024),
        cost_estimate=cost(20),
    )(table, a_tiles, left, own, right)


def coarsest_body(table, *refs):
    parts = refs[:PAIRS]
    high_ref, low_ref, out_ref, right, rest, left, left_rest, applied, applied_rest, held, q_sem, part_sem = refs[PAIRS:]

    def block_at(u, v):
        u, v = lax.bitwise_and(table[2, INFO] + u, 3), lax.bitwise_and(table[3, INFO] + v, 3)
        block = jnp.where(table[1, INFO] == 0, u * SIDE + v, v * SIDE + u)
        return pl.ds(pl.multiple_of(block * TILE, TILE), TILE)

    factors = [
        pltpu.make_async_copy(src.at[n], dst.at[block_at(n % SIDE, n // SIDE)], q_sem.at[m])
        for m, (src, dst) in enumerate(((high_ref, right), (low_ref, rest)))
        for n in range(CBS)
    ]
    loads = [
        pltpu.make_async_copy(part, held.at[pl.ds(2 * n, 2)], part_sem.at[n]) for n, part in enumerate(parts)
    ]
    for copy in factors[:CBS] + loads[:4] + factors[CBS:]:
        copy.start()
    for m, (src, dst) in enumerate(((high_ref, right), (low_ref, rest))):
        pltpu.make_async_copy(src, dst.reshape(CBS, TILE, C2), q_sem.at[m]).wait()
    for n, code in enumerate(SEQUENCE):
        place, columns = block_at(code // SIDE, code % SIDE), pl.ds(n * TILE, TILE)
        left[:, columns] = right[place, :].T
        left_rest[:, columns] = rest[place, :].T
    for n in range(PAIRS):
        loads[n].wait()
        if n + 4 < PAIRS:
            loads[n + 4].start()
        for m in (2 * n, 2 * n + 1):
            value = jnp.dot(held[m], right[...], preferred_element_type=jnp.float32)
            high = value.astype(jnp.bfloat16)
            rows = pl.ds(m * TILE, TILE)
            applied[rows, :] = high
            applied_rest[rows, :] = (value - high.astype(jnp.float32)).astype(jnp.bfloat16)
    for first in range(0, C2, TILE):
        rows = pl.ds(first, TILE)
        term = jnp.dot(left[rows, :], applied[...], preferred_element_type=jnp.float32)
        term += jnp.dot(left[rows, :], applied_rest[...], preferred_element_type=jnp.float32)
        term += jnp.dot(left_rest[rows, :], applied[...], preferred_element_type=jnp.float32)
        out_ref[rows, :] = term


def coarsest_term(table, parts, high, low):
    return pl.pallas_call(
        coarsest_body,
        out_shape=jax.ShapeDtypeStruct((C2, C2), jnp.float32),
        grid_spec=pltpu.PrefetchScalarGridSpec(
            num_scalar_prefetch=1,
            grid=(1,),
            in_specs=[pl.BlockSpec(memory_space=pl.ANY)] * (PAIRS + 2),
            out_specs=pl.BlockSpec((C2, C2), lambda j, *_: (0, 0)),
            scratch_shapes=[
                pltpu.VMEM((WIDTH, C2), jnp.bfloat16),
                pltpu.VMEM((WIDTH, C2), jnp.bfloat16),
                pltpu.VMEM((C2, WIDTH), jnp.bfloat16),
                pltpu.VMEM((C2, WIDTH), jnp.bfloat16),
                pltpu.VMEM((WIDTH, C2), jnp.bfloat16),
                pltpu.VMEM((WIDTH, C2), jnp.bfloat16),
                pltpu.VMEM((2 * PAIRS, TILE, WIDTH), jnp.bfloat16),
                pltpu.SemaphoreType.DMA((2,)),
                pltpu.SemaphoreType.DMA((PAIRS,)),
            ],
        ),
        compiler_params=pltpu.CompilerParams(vmem_limit_bytes=52 * 1024 * 1024),
        cost_estimate=cost(6),
    )(table, *parts, high, low)


def held_back(first, second, after_this):
    anywhere = pl.BlockSpec(memory_space=pl.ANY)
    return pl.pallas_call(
        lambda *refs: None,
        out_shape=[jax.ShapeDtypeStruct(value.shape, value.dtype) for value in (first, second)],
        in_specs=[anywhere] * 3,
        out_specs=[anywhere] * 2,
        input_output_aliases={0: 0, 1: 1},
        cost_estimate=cost(1),
    )(first, second, after_this)


def joined_body(up, from_far_a, down, from_far_b, _, up_out, down_out):
    up_out[...] = (up[...].astype(jnp.float32) + from_far_a[...].astype(jnp.float32)).astype(jnp.bfloat16)
    down_out[...] = (down[...].astype(jnp.float32) + from_far_b[...].astype(jnp.float32)).astype(jnp.bfloat16)


def joined(up, from_far_a, down, from_far_b, after_this):
    rows = 32
    part = pl.BlockSpec((2, rows, WIDTH), lambda j: (0, j, 0))
    return pl.pallas_call(
        joined_body,
        out_shape=[jax.ShapeDtypeStruct(up.shape, jnp.bfloat16)] * 2,
        grid=(TILE // rows,),
        in_specs=[part] * 4 + [pl.BlockSpec(memory_space=pl.ANY)],
        out_specs=[part] * 2,
        compiler_params=pltpu.CompilerParams(vmem_limit_bytes=32 * 1024 * 1024),
        cost_estimate=cost(2),
    )(up, from_far_a, down, from_far_b, after_this)


def torus_steps():
    def pairs(second, target):
        found = []
        for sect in range(8):
            for row in range(SIDE * SIDE):
                at = [row // SIDE, row % SIDE]
                axis = (sect % 2) ^ second
                at[axis] = target(at[axis])
                found.append((sect * 16 + row, sect * 16 + at[0] * SIDE + at[1]))
        return found

    return [{by: pairs(second, lambda at: (at + by) % SIDE) for by in (1, -1, 2)} for second in (0, 1)]


STEPS = torus_steps()


def send(value, second, by):
    return lax.ppermute(value, ("sect", "rows"), STEPS[second][by])


def wide(value):
    return value.astype(jnp.float32)


def share_out(term):
    pieces = term.reshape(32, 8, 2, 128).transpose(0, 2, 1, 3).reshape(128, 4, 128)
    return jnp.sum(lax.all_to_all(pieces, ("sect", "rows"), 0, 0), axis=0)


def bring_back(piece):
    back = lax.all_to_all(jnp.broadcast_to(piece[None], (128,) + piece.shape), ("sect", "rows"), 0, 0)
    return back.reshape(32, 2, 8, 128).transpose(0, 2, 1, 3).reshape(C2, C2)


def around(value, second):
    return jnp.stack([value, send(value, second, -1), send(value, second, 2), send(value, second, 1)])


def reduced_body(own_a, own_b, up_a, up_b, down_a, down_b, _, far, after, before, mine):
    def total(n, *refs):
        value = refs[0][n].astype(jnp.float32)
        for ref in refs[1:]:
            value = value + ref[n].astype(jnp.float32)
        return value

    far[...] = total(0, own_a, up_a, down_a).astype(jnp.bfloat16)
    after[...] = total(1, own_a, up_a, down_a).astype(jnp.bfloat16)
    before[...] = total(0, own_b, up_b, down_b).astype(jnp.bfloat16)
    mine[...] = total(1, own_b, up_b, down_b)


def reduced(own_a, own_b, up_a, up_b, down_a, down_b, after_this):
    rows = 32
    pair = pl.BlockSpec((2, rows, WIDTH), lambda j: (0, j, 0))
    one = pl.BlockSpec((rows, WIDTH), lambda j: (j, 0))
    shape = (TILE, WIDTH)
    return pl.pallas_call(
        reduced_body,
        out_shape=[jax.ShapeDtypeStruct(shape, jnp.bfloat16)] * 3 + [jax.ShapeDtypeStruct(shape, jnp.float32)],
        grid=(TILE // rows,),
        in_specs=[pair] * 6 + [pl.BlockSpec(memory_space=pl.ANY)],
        out_specs=[one] * 4,
        compiler_params=pltpu.CompilerParams(vmem_limit_bytes=32 * 1024 * 1024),
        cost_estimate=cost(3),
    )(own_a, own_b, up_a, up_b, down_a, down_b, after_this)


def per_device(a_tiles, a_cols, a_count, p_tiles, coarse_map, p_coarse):
    section = lax.axis_index("sect")
    position = lax.axis_index("rows")
    core = lax.rem(section, 2)
    x, y = lax.div(position, SIDE), lax.rem(position, SIDE)
    u, v = jnp.where(core == 0, x, y), jnp.where(core == 0, y, x)
    zero = jnp.zeros_like(core)
    first_row = (section * 16 + position - 1) * RB
    info = jnp.stack([section * CBS, core, u, v, first_row, zero, zero, zero]).astype(jnp.int32)
    up = [(i, i + 1) for i in range(15)]
    down = [(i + 1, i) for i in range(15)]
    local_map = coarse_map - section * CBS
    map_tile = jnp.pad(local_map.astype(jnp.bfloat16)[None, None], ((0, 0), (0, TILE - 1), (0, TILE - RB)))
    own = jnp.concatenate([p_tiles, map_tile], axis=0)
    left, right = lax.ppermute(own, "rows", up), lax.ppermute(own, "rows", down)
    maps = jnp.stack([left[RB, 0, :RB].astype(jnp.int32), local_map, right[RB, 0, :RB].astype(jnp.int32)])

    line = around((p_coarse * Q_SCALE).astype(jnp.float16), 0)
    square = around(line, 1)
    table = jnp.concatenate([row_plan(a_cols, a_count, coarse_map, info), jnp.pad(maps, ((0, 0), (0, 32 - RB)))], axis=0)
    *parts, scale = galerkin(table, a_tiles, left, own, right)
    far_a, far_b, up_b, down_a, up_a, down_b, own_a, own_b = parts
    prolong = square.reshape(CBS, TILE, C2).astype(jnp.float32) * scale[0, 0]
    prolong_high = lax.reduce_precision(prolong, 8, 7)
    prolong_low = (prolong - prolong_high).astype(jnp.bfloat16)
    prolong_high = prolong_high.astype(jnp.bfloat16)
    square_held = jnp.sum(square[1:, 0, :8, :TILE].astype(jnp.float32) * scale, axis=0)
    far_a, far_b = held_back(far_a, far_b, square_held)
    parts = (far_a, far_b, up_b, down_a, up_a, down_b, own_a, own_b)
    from_far_a, from_far_b = send(far_a, 0, 1), send(far_b, 0, -1)
    from_up_b, from_down_a = send(up_b, 0, 1), send(down_a, 0, -1)
    own_term = coarsest_term(table, parts, prolong_high, prolong_low)
    up_a, down_b = joined(up_a, from_far_a, down_b, from_far_b, own_term)
    from_up_a, from_down_b = send(up_a, 0, 1), send(down_b, 0, -1)

    own_piece = share_out(own_term)
    far, after, before, mine = reduced(own_a, own_b, from_up_a, from_up_b, from_down_a, from_down_b, own_piece)
    from_far, from_after, from_before = send(far, 1, 2), send(after, 1, 1), send(before, 1, -1)
    coarsest = bring_back(own_piece)
    owned_rows = mine + (wide(from_far) + (wide(from_after) + wide(from_before)))
    return (owned_rows, coarsest)


def solution(mesh):
    placed = (
        P(("sect", "rows"), None, None, None),
        P(("sect", "rows"), None),
        P(("sect", "rows")),
        P(("sect", "rows"), None, None),
        P(("sect", "rows")),
        P(("sect", "rows"), None),
    )
    return jax.shard_map(
        per_device,
        mesh=mesh,
        in_specs=placed,
        out_specs=(P(("sect", "rows"), None), P()),
        check_vma=False,
    )
```

```python
import functools

import jax
import jax.numpy as jnp
from jax import lax
from jax.experimental import pallas as pl
from jax.experimental.pallas import tpu as pltpu
from jax.sharding import PartitionSpec as P

CBS = 16
TILE = 128
RB = 16
KA = 27
GROUP = 2
AHEAD = 3
CUTS = 3
STAGES = 4
SIDE = 4
WIDTH = CBS * TILE
C2 = 256

HALF_A = (2, 1)
HALF_B = (3, 0)
FAR = [2 * SIDE + dv for dv in HALF_A + HALF_B]
NEXT_ALONE = [1 * SIDE + dv for dv in HALF_B] + [3 * SIDE + dv for dv in HALF_A]
OWN = [0 * SIDE + dv for dv in HALF_A + HALF_B]
NEXT_JOINED = [1 * SIDE + dv for dv in HALF_A] + [3 * SIDE + dv for dv in HALF_B]
SEQUENCE = FAR + NEXT_ALONE + NEXT_JOINED + OWN
PAIRS = len(SEQUENCE) // 2
COUNT, ORDER, STARTS, INFO = KA, KA + 1, KA + 2, KA + 3
Q_SCALE = 2.0**20


def cost(microseconds):
    return pl.CostEstimate(flops=0, bytes_accessed=int(microseconds * 3.7e6), transcendentals=0)


def plan_body(cols, counts, own_map, info, table):
    def fill(i, _):
        for k in range(KA):
            table[i, k] = cols[i, k] - info[4]
        table[i, COUNT] = counts[i]
        table[i, INFO] = info[lax.min(i, 7)]
        return 0

    lax.fori_loop(0, RB, fill, 0)
    first_core = info[1] == 0
    names = []
    for i in range(RB):
        block = own_map[i] - info[0]
        high, low = lax.shift_right_logical(block, 2), lax.bitwise_and(block, 3)
        du = lax.bitwise_and(jnp.where(first_core, high, low) - info[2], 3)
        dv = lax.bitwise_and(jnp.where(first_core, low, high) - info[3], 3)
        names.append(du * SIDE + dv)
    n = jnp.int32(0)
    for j, code in enumerate(SEQUENCE):
        table[j, STARTS] = n
        for i in range(RB):
            table[n, ORDER] = jnp.int32(i)
            n = n + (names[i] == code).astype(jnp.int32)
    table[len(SEQUENCE), STARTS] = n


def row_plan(*operands):
    smem = pl.BlockSpec(memory_space=pltpu.SMEM)
    return pl.pallas_call(
        plan_body,
        out_shape=jax.ShapeDtypeStruct((RB + 1, 32), jnp.int32),
        in_specs=[smem] * len(operands),
        out_specs=smem,
        cost_estimate=cost(3),
    )(*operands)


def galerkin_body(table, maps, a_ref, left_ref, own_ref, right_ref, *rest):
    outs, (scale_ref, a_buf, tiles, acc, stage, a_sem, p_sem, out_sem) = rest[:PAIRS], rest[PAIRS:]
    scale_ref[...] = jnp.full(scale_ref.shape, 1.0 / Q_SCALE, jnp.float32)

    def fetch(r):
        slot = lax.rem(r, AHEAD + 1)
        part = KA // CUTS
        return [
            pltpu.make_async_copy(
                a_ref.at[table[r, ORDER], pl.ds(n * part, part)], a_buf.at[slot, pl.ds(n * part, part)], a_sem.at[slot, n]
            )
            for n in range(CUTS)
        ]

    loads = [
        pltpu.make_async_copy(src.at[pl.ds(0, RB)], tiles.at[pl.ds(n * RB, RB)], p_sem.at[n])
        for n, src in enumerate((left_ref, own_ref, right_ref))
    ]
    for load in loads:
        load.start()
    for r in range(AHEAD):
        for copy in fetch(r):
            copy.start()
    acc[...] = jnp.zeros_like(acc)
    for load in loads:
        load.wait()

    def row(r, _):
        @pl.when(r + AHEAD < RB)
        def _():
            for copy in fetch(r + AHEAD):
                copy.start()

        for copy in fetch(r):
            copy.wait()
        i = table[r, ORDER]
        slot = lax.rem(r, AHEAD + 1)
        count = table[i, COUNT]
        left = tiles[RB + i].T
        for k in range(0, KA, GROUP):
            products, places = [], []
            for s in range(k, min(k + GROUP, KA)):
                col = jnp.clip(table[i, s], 0, 3 * RB - 1)
                block = jnp.clip(maps[lax.shift_right_logical(col, 4), lax.bitwise_and(col, RB - 1)], 0, CBS - 1)
                places.append(pl.multiple_of(jnp.where(s < count, block, CBS) * TILE, TILE))
                products.append(
                    jnp.dot(a_buf[slot, s], tiles[col], preferred_element_type=jnp.float32).astype(jnp.bfloat16)
                )
            terms = jnp.dot(left, jnp.concatenate(products, axis=1) if len(products) > 1 else products[0], preferred_element_type=jnp.float32)
            for n, place in enumerate(places):
                acc[:, pl.ds(place, TILE)] += terms[:, n * TILE:(n + 1) * TILE]
        return 0

    def leave(n, half, slot):
        return pltpu.make_async_copy(stage.at[slot], outs[n].at[half], out_sem.at[slot])

    def block(t, _):
        pair, half, slot = lax.div(t, 2), lax.rem(t, 2), lax.rem(t, STAGES)
        lax.fori_loop(table[t, STARTS], table[t + 1, STARTS], row, 0)

        @pl.when(t >= STAGES)
        def _():
            leave(0, 0, slot).wait()

        for first in range(0, WIDTH, TILE):
            columns = pl.ds(first, TILE)
            stage[slot, :, columns] = acc[:, columns].astype(jnp.bfloat16)
            acc[:, columns] = jnp.zeros((TILE, TILE), jnp.float32)
        for n in range(PAIRS):
            @pl.when(pair == n)
            def _(n=n):
                leave(n, half, slot).start()
        return 0

    lax.fori_loop(0, 2 * PAIRS, block, 0)
    for slot in range(STAGES):
        leave(0, 0, slot).wait()


def galerkin(table, maps, a_tiles, left, own, right):
    anywhere = pl.BlockSpec(memory_space=pl.ANY)
    return pl.pallas_call(
        galerkin_body,
        out_shape=[jax.ShapeDtypeStruct((2, TILE, WIDTH), jnp.bfloat16)] * PAIRS
        + [jax.ShapeDtypeStruct((1, TILE), jnp.float32)],
        grid_spec=pltpu.PrefetchScalarGridSpec(
            num_scalar_prefetch=2,
            grid=(1,),
            in_specs=[pl.BlockSpec(memory_space=pltpu.HBM)] + [anywhere] * 3,
            out_specs=[anywhere] * PAIRS + [pl.BlockSpec((1, TILE), lambda j, *_: (0, 0))],
            scratch_shapes=[
                pltpu.VMEM((AHEAD + 1, KA, TILE, TILE), jnp.bfloat16),
                pltpu.VMEM((3 * RB, TILE, TILE), jnp.bfloat16),
                pltpu.VMEM((TILE, WIDTH + TILE), jnp.float32),
                pltpu.VMEM((STAGES, TILE, WIDTH), jnp.bfloat16),
                pltpu.SemaphoreType.DMA((AHEAD + 1, CUTS)),
                pltpu.SemaphoreType.DMA((3,)),
                pltpu.SemaphoreType.DMA((STAGES,)),
            ],
        ),
        compiler_params=pltpu.CompilerParams(vmem_limit_bytes=52 * 1024 * 1024),
        cost_estimate=cost(20),
    )(table, maps, a_tiles, left, own, right)


def coarsest_body(table, *refs):
    parts = refs[:PAIRS]
    high_ref, low_ref, out_ref, right, rest, left, left_rest, applied, applied_rest, held, q_sem, part_sem = refs[PAIRS:]

    def block_at(u, v):
        u, v = lax.bitwise_and(table[2, INFO] + u, 3), lax.bitwise_and(table[3, INFO] + v, 3)
        block = jnp.where(table[1, INFO] == 0, u * SIDE + v, v * SIDE + u)
        return pl.ds(pl.multiple_of(block * TILE, TILE), TILE)

    factors = [
        pltpu.make_async_copy(src.at[n], dst.at[block_at(n % SIDE, n // SIDE)], q_sem.at[m])
        for m, (src, dst) in enumerate(((high_ref, right), (low_ref, rest)))
        for n in range(CBS)
    ]
    loads = [
        pltpu.make_async_copy(part, held.at[pl.ds(2 * n, 2)], part_sem.at[n]) for n, part in enumerate(parts)
    ]
    for copy in factors[:CBS] + loads[:4] + factors[CBS:]:
        copy.start()
    for m, (src, dst) in enumerate(((high_ref, right), (low_ref, rest))):
        pltpu.make_async_copy(src, dst.reshape(CBS, TILE, C2), q_sem.at[m]).wait()
    for n, code in enumerate(SEQUENCE):
        place, columns = block_at(code // SIDE, code % SIDE), pl.ds(n * TILE, TILE)
        left[:, columns] = right[place, :].T
        left_rest[:, columns] = rest[place, :].T
    for n in range(PAIRS):
        loads[n].wait()
        if n + 4 < PAIRS:
            loads[n + 4].start()
        for m in (2 * n, 2 * n + 1):
            value = jnp.dot(held[m], right[...], preferred_element_type=jnp.float32)
            high = value.astype(jnp.bfloat16)
            rows = pl.ds(m * TILE, TILE)
            applied[rows, :] = high
            applied_rest[rows, :] = (value - high.astype(jnp.float32)).astype(jnp.bfloat16)
    for first in range(0, C2, TILE):
        rows = pl.ds(first, TILE)
        term = jnp.dot(left[rows, :], applied[...], preferred_element_type=jnp.float32)
        term += jnp.dot(left[rows, :], applied_rest[...], preferred_element_type=jnp.float32)
        term += jnp.dot(left_rest[rows, :], applied[...], preferred_element_type=jnp.float32)
        out_ref[rows, :] = term


def coarsest_term(table, parts, high, low):
    return pl.pallas_call(
        coarsest_body,
        out_shape=jax.ShapeDtypeStruct((C2, C2), jnp.float32),
        grid_spec=pltpu.PrefetchScalarGridSpec(
            num_scalar_prefetch=1,
            grid=(1,),
            in_specs=[pl.BlockSpec(memory_space=pl.ANY)] * (PAIRS + 2),
            out_specs=pl.BlockSpec((C2, C2), lambda j, *_: (0, 0)),
            scratch_shapes=[
                pltpu.VMEM((WIDTH, C2), jnp.bfloat16),
                pltpu.VMEM((WIDTH, C2), jnp.bfloat16),
                pltpu.VMEM((C2, WIDTH), jnp.bfloat16),
                pltpu.VMEM((C2, WIDTH), jnp.bfloat16),
                pltpu.VMEM((WIDTH, C2), jnp.bfloat16),
                pltpu.VMEM((WIDTH, C2), jnp.bfloat16),
                pltpu.VMEM((2 * PAIRS, TILE, WIDTH), jnp.bfloat16),
                pltpu.SemaphoreType.DMA((2,)),
                pltpu.SemaphoreType.DMA((PAIRS,)),
            ],
        ),
        compiler_params=pltpu.CompilerParams(vmem_limit_bytes=52 * 1024 * 1024),
        cost_estimate=cost(6),
    )(table, *parts, high, low)


def held_back(first, second, after_this):
    anywhere = pl.BlockSpec(memory_space=pl.ANY)
    return pl.pallas_call(
        lambda *refs: None,
        out_shape=[jax.ShapeDtypeStruct(value.shape, value.dtype) for value in (first, second)],
        in_specs=[anywhere] * 3,
        out_specs=[anywhere] * 2,
        input_output_aliases={0: 0, 1: 1},
        cost_estimate=cost(1),
    )(first, second, after_this)


def joined_body(up, from_far_a, down, from_far_b, _, up_out, down_out):
    up_out[...] = (up[...].astype(jnp.float32) + from_far_a[...].astype(jnp.float32)).astype(jnp.bfloat16)
    down_out[...] = (down[...].astype(jnp.float32) + from_far_b[...].astype(jnp.float32)).astype(jnp.bfloat16)


def joined(up, from_far_a, down, from_far_b, after_this):
    rows = 64
    part = pl.BlockSpec((2, rows, WIDTH), lambda j: (0, j, 0))
    return pl.pallas_call(
        joined_body,
        out_shape=[jax.ShapeDtypeStruct(up.shape, jnp.bfloat16)] * 2,
        grid=(TILE // rows,),
        in_specs=[part] * 4 + [pl.BlockSpec(memory_space=pl.ANY)],
        out_specs=[part] * 2,
        compiler_params=pltpu.CompilerParams(vmem_limit_bytes=32 * 1024 * 1024),
        cost_estimate=cost(2),
    )(up, from_far_a, down, from_far_b, after_this)


def torus_steps():
    def pairs(second, target):
        found = []
        for sect in range(8):
            for row in range(SIDE * SIDE):
                at = [row // SIDE, row % SIDE]
                axis = (sect % 2) ^ second
                at[axis] = target(at[axis])
                found.append((sect * 16 + row, sect * 16 + at[0] * SIDE + at[1]))
        return found

    return [{by: pairs(second, lambda at: (at + by) % SIDE) for by in (1, -1, 2)} for second in (0, 1)]


STEPS = torus_steps()


def send(value, second, by):
    return lax.ppermute(value, ("sect", "rows"), STEPS[second][by])


def wide(value):
    return value.astype(jnp.float32)


def share_out(term):
    pieces = term.reshape(32, 8, 2, 128).transpose(0, 2, 1, 3).reshape(128, 4, 128)
    return jnp.sum(lax.all_to_all(pieces, ("sect", "rows"), 0, 0), axis=0)


def bring_back(piece):
    back = lax.all_to_all(jnp.broadcast_to(piece[None], (128,) + piece.shape), ("sect", "rows"), 0, 0)
    return back.reshape(32, 2, 8, 128).transpose(0, 2, 1, 3).reshape(C2, C2)


def around(value, second):
    return jnp.stack([value, send(value, second, -1), send(value, second, 2), send(value, second, 1)])


def reduced_body(own_a, own_b, up_a, up_b, down_a, down_b, _, far, after, before, mine):
    def total(n, *refs):
        value = refs[0][n].astype(jnp.float32)
        for ref in refs[1:]:
            value = value + ref[n].astype(jnp.float32)
        return value

    far[...] = total(0, own_a, up_a, down_a).astype(jnp.bfloat16)
    after[...] = total(1, own_a, up_a, down_a).astype(jnp.bfloat16)
    before[...] = total(0, own_b, up_b, down_b).astype(jnp.bfloat16)
    mine[...] = total(1, own_b, up_b, down_b)


def reduced(own_a, own_b, up_a, up_b, down_a, down_b, after_this):
    rows = 128
    pair = pl.BlockSpec((2, rows, WIDTH), lambda j: (0, j, 0))
    one = pl.BlockSpec((rows, WIDTH), lambda j: (j, 0))
    shape = (TILE, WIDTH)
    return pl.pallas_call(
        reduced_body,
        out_shape=[jax.ShapeDtypeStruct(shape, jnp.bfloat16)] * 3 + [jax.ShapeDtypeStruct(shape, jnp.float32)],
        grid=(TILE // rows,),
        in_specs=[pair] * 6 + [pl.BlockSpec(memory_space=pl.ANY)],
        out_specs=[one] * 4,
        compiler_params=pltpu.CompilerParams(vmem_limit_bytes=32 * 1024 * 1024),
        cost_estimate=cost(3),
    )(own_a, own_b, up_a, up_b, down_a, down_b, after_this)


def per_device(a_tiles, a_cols, a_count, p_tiles, coarse_map, p_coarse):
    section = lax.axis_index("sect")
    position = lax.axis_index("rows")
    core = lax.rem(section, 2)
    x, y = lax.div(position, SIDE), lax.rem(position, SIDE)
    u, v = jnp.where(core == 0, x, y), jnp.where(core == 0, y, x)
    zero = jnp.zeros_like(core)
    first_row = (section * 16 + position - 1) * RB
    info = jnp.stack([section * CBS, core, u, v, first_row, zero, zero, zero]).astype(jnp.int32)
    up = [(i, i + 1) for i in range(15)]
    down = [(i + 1, i) for i in range(15)]
    local_map = coarse_map - section * CBS
    map_tile = jnp.pad(local_map.astype(jnp.bfloat16)[None, None], ((0, 0), (0, TILE - 1), (0, TILE - RB)))
    own = jnp.concatenate([p_tiles, map_tile], axis=0)
    left, right = lax.ppermute(own, "rows", up), lax.ppermute(own, "rows", down)
    maps = jnp.stack([left[RB, 0, :RB].astype(jnp.int32), local_map, right[RB, 0, :RB].astype(jnp.int32)])

    line = around((p_coarse * Q_SCALE).astype(jnp.float16), 0)
    square = around(line, 1)
    table = row_plan(a_cols, a_count, coarse_map, info)
    *parts, scale = galerkin(table, maps, a_tiles, left, own, right)
    far_a, far_b, up_b, down_a, up_a, down_b, own_a, own_b = parts
    prolong = square.reshape(CBS, TILE, C2).astype(jnp.float32) * scale[0, 0]
    prolong_high = lax.reduce_precision(prolong, 8, 7)
    prolong_low = (prolong - prolong_high).astype(jnp.bfloat16)
    prolong_high = prolong_high.astype(jnp.bfloat16)
    square_held = jnp.sum(square[1:, 0, :8, :TILE].astype(jnp.float32) * scale, axis=0)
    far_a, far_b = held_back(far_a, far_b, square_held)
    parts = (far_a, far_b, up_b, down_a, up_a, down_b, own_a, own_b)
    from_far_a, from_far_b = send(far_a, 0, 1), send(far_b, 0, -1)
    from_up_b, from_down_a = send(up_b, 0, 1), send(down_a, 0, -1)
    own_term = coarsest_term(table, parts, prolong_high, prolong_low)
    up_a, down_b = joined(up_a, from_far_a, down_b, from_far_b, own_term)
    from_up_a, from_down_b = send(up_a, 0, 1), send(down_b, 0, -1)

    own_piece = share_out(own_term)
    far, after, before, mine = reduced(own_a, own_b, from_up_a, from_up_b, from_down_a, from_down_b, own_piece)
    from_far, from_after, from_before = send(far, 1, 2), send(after, 1, 1), send(before, 1, -1)
    coarsest = bring_back(own_piece)
    owned_rows = mine + (wide(from_far) + (wide(from_after) + wide(from_before)))
    return (owned_rows, coarsest)


def solution(mesh):
    placed = (
        P(("sect", "rows"), None, None, None),
        P(("sect", "rows"), None),
        P(("sect", "rows")),
        P(("sect", "rows"), None, None),
        P(("sect", "rows")),
        P(("sect", "rows"), None),
    )
    return jax.shard_map(
        per_device,
        mesh=mesh,
        in_specs=placed,
        out_specs=(P(("sect", "rows"), None), P()),
        check_vma=False,
    )
```
